32 devices in a mesh: groups: 2 (over y), graph: 16 (over z, x, core).
Axes of the slice: x: 2, y: 2, z: 4, core: 2. Of those that a mesh axis runs over, the one named last changes fastest.
Arguments:
- edge_state: bfloat16 [8192, 512], P(('groups', 'graph')), parts along dimension 0, may hold values from -6 to 6
- atom_state: bfloat16 [512, 256], P(('groups', 'graph')), parts along dimension 0, may hold values from -6 to 6
- atom_sends: int32 [4096], P(('groups', 'graph')), parts along dimension 0, may hold values from 0 to 15
- edge_source: int32 [8192], P(('groups', 'graph')), parts along dimension 0, may hold values from 0 to 127
- edge_target: int32 [8192], P(('groups', 'graph')), parts along dimension 0, may hold values from 0 to 15
- send_edges: int32 [262144], P(('groups', 'graph')), parts along dimension 0, may hold values from 0 to 255
- triplet_in: int32 [262144], P(('groups', 'graph')), parts along dimension 0, may hold values from 0 to 8191, as said below
- triplet_out: int32 [262144], P(('groups', 'graph')), parts along dimension 0, may hold values from 0 to 8191, as said below
- triplet_valid: int32 [262144], P(('groups', 'graph')), parts along dimension 0, may hold values 0 or 1
- triplet_basis: bfloat16 [16, 262144], P(None, ('groups', 'graph')), parts along dimension 1, may hold values from -6 to 6
- return_edges: int32 [262144], P(('groups', 'graph')), parts along dimension 0, may hold values from 0 to 255
- w_edge: bfloat16 [512, 512], replicated, may hold values from -0.25 to 0.25
- w_source: bfloat16 [256, 512], replicated, may hold values from -0.375 to 0.375
- w_down: bfloat16 [512, 64], replicated, may hold values from -0.25 to 0.25
- w_bilinear: bfloat16 [64, 1024], replicated, may hold values from -0.1875 to 0.1875
- w_up: bfloat16 [64, 512], replicated, may hold values from -0.125 to 0.125
- w_residual: bfloat16 [4, 512, 512], replicated, may hold values from -0.25 to 0.25
- w_atom: bfloat16 [512, 256], replicated, may hold values from -0.25 to 0.25
Outputs:
- edge_out: bfloat16 [8192, 512], P(('groups', 'graph')), parts along dimension 0
- atom_out: bfloat16 [512, 256], P(('groups', 'graph')), parts along dimension 0
The draws below stay inside these ranges and needn't reach their ends.
There are 2 independent parts, one for each index of `groups`. The reference program is written for one: setup_inputs(seed, part) draws one part's arguments, and reference() takes and returns one part's arrays. A program takes and returns all parts, laid end to end along the dimension named above; an argument that names none is the same for every part. Nothing has to cross between parts.
Inputs may be any that keep to these rules, and one draw needn't show every extreme that they name: `atom_sends`: entry d * 8 + c of a device's 128 entries is sent to device d. `send_edges`: entry t * 512 + c of a device's 8192 entries is sent to tile t. `triplet_in`: triplet j of a tile reads a received slot in the same aligned block of 512 slots as j. `triplet_out`: slot d * 512 + c of a tile is returned to device d; triplet j of a tile adds to a slot in the same aligned block of 512 slots as j. `return_edges`: entry t * 512 + c of a device's 8192 entries belongs to the slot that tile t returns in place c.
All inputs are finite; a program needn't handle non-finite values. No bound on the sum of `triplet_valid` on one device may be relied on, other than what follows from the above.
Results may differ from the reference program's by a relative error of at most 0.0095.
Values may be sent and summed in bfloat16 or wider, within the bound.
No kernel may reach another device: no remote copies, remote signals or barrier semaphores. Data moves between devices by JAX's collectives and lax.ppermute only.
A program may use at most 64 MiB of HBM per device.

```python
import jax
import jax.numpy as jnp
from jax import lax

DE = 512
DA = 256
DP = 64
NB = 16
E_DEV = 256
TPE = 32
WIN = 512
ATOM_DEV = 16
EDGES = 4096
ATOMS = 256
TRIP_DEV = 8192
TRIPLETS = 131072
CAP = 512
ASLOTS = 128
CAP_A = 8
ASENDS = 2048
N_GRAPH = 16


def block_slots(key):
    positions = jnp.arange(TRIPLETS, dtype=jnp.int32) % TRIP_DEV
    starts = positions // WIN * WIN
    return starts + jax.random.randint(key, (TRIPLETS,), 0, WIN, dtype=jnp.int32)


def draw_triplet_in(key, part):
    return block_slots(jax.random.fold_in(key, 101))


def draw_triplet_out(key, part):
    return block_slots(jax.random.fold_in(key, 202))


def touch_ends(entries, key, smallest, high):
    longest = entries.shape.index(max(entries.shape))
    spots = []
    for shift in (0, 1):
        where = [jax.random.randint(jax.random.fold_in(key, axis), (), 0, length) for axis, length in enumerate(entries.shape)]
        where[longest] = (where[longest] + shift) % entries.shape[longest]
        spots.append(tuple(where))
    return entries.at[spots[0]].set(smallest).at[spots[1]].set(high)


def block_levels(own_key, dims, cuts, low, top_value):
    factor_of, own = 1.0, jax.random.fold_in(own_key, 6)
    for dim, shards_of in cuts:
        steps = jnp.exp(jax.random.uniform(jax.random.fold_in(own, dim), (shards_of,), jnp.float32, low / len(cuts), top_value / len(cuts)))
        factor_of = factor_of * jnp.repeat(steps, dims[dim] // shards_of).reshape([-1 if axis == dim else 1 for axis in range(len(dims))])
    return factor_of


def bell_draw(rng, dims, scale, most, pieces=(), kind=jnp.bfloat16):
    gain = block_levels(rng, dims, pieces, -0.22, 0.18) if pieces else 1.0
    entries = jax.random.normal(rng, dims, jnp.float32) * scale * gain
    return jnp.minimum(jnp.maximum(entries, -most), most).astype(kind)


def setup_inputs(seed: int = 0, part: int = 0) -> dict:
    streams_of = jax.random.split(jax.random.key(seed), 19)
    own_keys = jax.random.split(jax.random.fold_in(streams_of[18], part), 19)
    return {
        "edge_state": bell_draw(own_keys[0], (EDGES, DE), 1.0, 6.0, ((0, 16),)),
        "atom_state": bell_draw(own_keys[1], (ATOMS, DA), 1.0, 6.0, ((0, 16),)),
        "atom_sends": touch_ends(jax.random.randint(own_keys[2], (ASENDS,), 0, ATOM_DEV), jax.random.fold_in(own_keys[2], 1), 0, ATOM_DEV - 1).astype(jnp.int32),
        "edge_source": touch_ends(jax.random.randint(own_keys[3], (EDGES,), 0, ASLOTS), jax.random.fold_in(own_keys[3], 1), 0, ASLOTS - 1).astype(jnp.int32),
        "edge_target": touch_ends(jax.random.randint(own_keys[4], (EDGES,), 0, ATOM_DEV), jax.random.fold_in(own_keys[4], 1), 0, ATOM_DEV - 1).astype(jnp.int32),
        "send_edges": touch_ends(jax.random.randint(own_keys[5], (TRIPLETS,), 0, E_DEV), jax.random.fold_in(own_keys[5], 1), 0, E_DEV - 1).astype(jnp.int32),
        "triplet_in": draw_triplet_in(jax.random.fold_in(jax.random.fold_in(streams_of[18], part), 71), part),
        "triplet_out": draw_triplet_out(jax.random.fold_in(jax.random.fold_in(streams_of[18], part), 71), part),
        "triplet_valid": touch_ends((jax.random.randint(own_keys[8], (TRIPLETS,), 0, 4) < 3).astype(jnp.int32), jax.random.fold_in(own_keys[8], 1), 0, 1),
        "triplet_basis": bell_draw(own_keys[9], (NB, TRIPLETS), 1.0, 6.0, ((1, 16),)),
        "return_edges": touch_ends(jax.random.randint(own_keys[10], (TRIPLETS,), 0, E_DEV), jax.random.fold_in(own_keys[10], 1), 0, E_DEV - 1).astype(jnp.int32),
        "w_edge": bell_draw(streams_of[11], (DE, DE), DE ** -0.5, 0.25),
        "w_source": bell_draw(streams_of[12], (DA, DE), DA ** -0.5, 0.375),
        "w_down": bell_draw(streams_of[13], (DE, DP), DE ** -0.5, 0.25),
        "w_bilinear": bell_draw(streams_of[14], (DP, NB * DP), (DP * NB) ** -0.5, 0.1875),
        "w_up": bell_draw(streams_of[15], (DP, DE), (DP * TPE) ** -0.5, 0.125),
        "w_residual": bell_draw(streams_of[16], (4, DE, DE), DE ** -0.5, 0.25),
        "w_atom": bell_draw(streams_of[17], (DE, DA), DE ** -0.5, 0.25),
    }


inv_root = 0.7071067811865476


def matmul(left, right):
    return jnp.dot(left, right, preferred_element_type=jnp.float32)


def bilinear_terms(inputs_x, coeffs, keeps, w_bilinear):
    expanded = matmul(inputs_x, w_bilinear)
    expanded = expanded.reshape(inputs_x.shape[0], coeffs.shape[0], -1)
    mixed = jnp.einsum("tkd,kt->td", expanded, coeffs.astype(jnp.float32))
    return mixed * keeps.astype(jnp.float32)[:, None]


def slot_table(indices, peer_count, width, shift):
    offsets = (jnp.arange(peer_count, dtype=jnp.int32) * shift)[:, None, None]
    shaped = indices.reshape(peer_count, peer_count, width) + offsets
    return jnp.transpose(shaped, (1, 0, 2)).reshape(peer_count, peer_count * width)


def reference(edge_state, atom_state, atom_sends, edge_source, edge_target, send_edges, triplet_in, triplet_out, triplet_valid, triplet_basis, return_edges, w_edge, w_source, w_down, w_bilinear, w_up, w_residual, w_atom):
    peer_count = N_GRAPH
    atom_slots = slot_table(atom_sends, peer_count, CAP_A, ATOM_DEV)
    source_ids = jnp.take_along_axis(atom_slots, edge_source.reshape(peer_count, E_DEV), axis=1).reshape(-1)
    src_rows = atom_state[source_ids]
    pre_act = matmul(edge_state, w_edge) + matmul(src_rows, w_source)
    activated = jax.nn.silu(pre_act).astype(jnp.bfloat16)
    projected = jax.nn.silu(matmul(activated, w_down)).astype(jnp.bfloat16)
    edge_slots = slot_table(send_edges, peer_count, CAP, E_DEV)
    back_slots = slot_table(return_edges, peer_count, CAP, E_DEV)

    def tile_work(operands):
        slot_ids, local_in, local_out, keeps, coeffs = operands
        inputs_x = projected[slot_ids[local_in]]
        mixed = bilinear_terms(inputs_x, coeffs, keeps, w_bilinear)
        summed = jnp.zeros((TRIP_DEV, DP), jnp.float32).at[local_out].add(mixed)
        return summed.astype(jnp.bfloat16)

    basis_tiles = jnp.transpose(triplet_basis.reshape(NB, peer_count, TRIP_DEV), (1, 0, 2))
    slot_sums = lax.map(tile_work, (edge_slots, triplet_in.reshape(peer_count, TRIP_DEV), triplet_out.reshape(peer_count, TRIP_DEV), triplet_valid.reshape(peer_count, TRIP_DEV), basis_tiles))
    aggregate = jnp.zeros((EDGES, DP), jnp.float32).at[back_slots.reshape(-1)].add(slot_sums.reshape(-1, DP).astype(jnp.float32))
    aggregate = aggregate.astype(jnp.bfloat16)
    update = jax.nn.silu(matmul(aggregate, w_up))
    base = ((edge_state.astype(jnp.float32) + activated.astype(jnp.float32)) * inv_root).astype(jnp.bfloat16)
    inner_one = jax.nn.silu(matmul(base, w_residual[0])).astype(jnp.bfloat16)
    middle = ((base.astype(jnp.float32) + jax.nn.silu(matmul(inner_one, w_residual[1]))) * inv_root).astype(jnp.bfloat16)
    inner_two = jax.nn.silu(matmul(middle, w_residual[2])).astype(jnp.bfloat16)
    chain = (middle.astype(jnp.float32) + jax.nn.silu(matmul(inner_two, w_residual[3]))) * inv_root
    edge_out = (chain + update).astype(jnp.bfloat16)
    contrib = matmul(edge_out, w_atom).astype(jnp.bfloat16)
    targets = edge_target + (jnp.arange(EDGES, dtype=jnp.int32) // E_DEV) * ATOM_DEV
    atom_sum = jnp.zeros((ATOMS, DA), jnp.float32).at[targets].add(contrib.astype(jnp.float32))
    atom_out = (atom_state.astype(jnp.float32) + jax.nn.silu(0.25 * atom_sum)).astype(jnp.bfloat16)
    return edge_out, atom_out
```

```python
import functools

import jax
import jax.numpy as jnp
from jax import lax
from jax.experimental import pallas as pl
from jax.experimental.pallas import tpu as pltpu
from jax.sharding import PartitionSpec as P

WIN = 512
LANES = 128


inv_root = 0.7071067811865476


def matmul(left, right):
    return jnp.dot(left, right, preferred_element_type=jnp.float32)


def pick_rows(indices, table):
    chooser = (indices[:, None] == jnp.arange(table.shape[0], dtype=jnp.int32)[None, :]).astype(
        table.dtype
    )
    return matmul(chooser, table).astype(table.dtype)


def silu(v):
    return (0.5 * v) * (1.0 + jnp.tanh(0.5 * v))


def pack_kernel(basis_ref, valid_ref, in_ref, out_ref, atom_ref, sends_ref, send_ref):
    basis_rows = basis_ref.shape[0]
    peers = send_ref.shape[0]
    pieces = valid_ref.shape[0] // peers
    width = pieces * LANES
    atom_slots = sends_ref.shape[1]
    cap_a = atom_slots // peers
    chooser = (
        lax.broadcasted_iota(jnp.int32, (atom_ref.shape[0], atom_slots), 0) == sends_ref[...]
    ).astype(jnp.float32).astype(jnp.bfloat16)
    rows = lax.dot_general(
        chooser, atom_ref[...], (((0,), (0,)), ((), ())), preferred_element_type=jnp.float32
    ).astype(jnp.bfloat16)
    keeps = valid_ref[...].astype(jnp.float32)
    half = width // 2
    local_in = ((in_ref[...] % width) - half).astype(jnp.float32).astype(jnp.bfloat16)
    local_out = ((out_ref[...] % width) - half).astype(jnp.float32).astype(jnp.bfloat16)
    for peer in range(peers):
        parts = []
        for piece in range(pieces):
            row = peer * pieces + piece
            tile = basis_ref[:, row * LANES : (row + 1) * LANES].astype(jnp.float32)
            parts.append((tile * keeps[row : row + 1, :]).astype(jnp.bfloat16))
        parts.append(local_in[peer * pieces : (peer + 1) * pieces, :])
        parts.append(local_out[peer * pieces : (peer + 1) * pieces, :])
        for first in range(0, atom_ref.shape[1], LANES):
            parts.append(rows[peer * cap_a : (peer + 1) * cap_a, first : first + LANES])
        send_ref[peer] = jnp.concatenate(parts, axis=0)


def main_kernel(
    recv_ref,
    edge_ref,
    atom_ref,
    source_ref,
    target_ref,
    send_ref,
    return_ref,
    w_edge_ref,
    w_source_ref,
    w_down_ref,
    w_bilinear_ref,
    w_up_ref,
    w_residual_ref,
    w_atom_ref,
    edge_out_ref,
    atom_out_ref,
):
    bf16, f32 = jnp.bfloat16, jnp.float32
    peers = recv_ref.shape[0]
    pieces = send_ref.shape[0] // peers
    width = pieces * LANES
    edge_count = edge_ref.shape[0]
    proj_width = w_down_ref.shape[1]
    basis_rows = w_bilinear_ref.shape[1] // proj_width
    index_row = basis_rows * pieces
    atom_row = index_row + 2 * pieces
    halves = atom_ref.shape[1] // LANES
    cap_a = (recv_ref.shape[1] - atom_row) // halves

    arrived = jnp.concatenate(
        [
            jnp.concatenate(
                [
                    recv_ref[s, atom_row + h * cap_a : atom_row + (h + 1) * cap_a, :]
                    for s in range(peers)
                ],
                axis=0,
            )
            for h in range(halves)
        ],
        axis=1,
    )
    source_hot = (
        lax.broadcasted_iota(jnp.int32, (arrived.shape[0], edge_count), 0) == source_ref[...]
    ).astype(f32).astype(bf16)
    src_rows = lax.dot_general(
        source_hot, arrived, (((0,), (0,)), ((), ())), preferred_element_type=f32
    ).astype(bf16)
    edge = edge_ref[...]
    activated = silu(matmul(edge, w_edge_ref[...]) + matmul(src_rows, w_source_ref[...])).astype(bf16)
    projected = silu(matmul(activated, w_down_ref[...])).astype(bf16)
    expanded = lax.dot_general(
        w_bilinear_ref[...], projected, (((0,), (1,)), ((), ())), preferred_element_type=f32
    ).astype(bf16)

    edge_iota = lax.broadcasted_iota(jnp.int32, (edge_count, LANES), 0).astype(f32).astype(bf16)
    upper = lax.broadcasted_iota(jnp.int32, (2 * pieces, LANES), 0) < pieces
    one, zero = jnp.ones((), bf16), jnp.zeros((), bf16)

    def one_hot(rows):
        parts = []
        for piece in range(pieces):
            spread = jnp.broadcast_to(rows[piece : piece + 1, :], (edge_count, LANES)).astype(bf16)
            parts.append(jnp.where(spread == edge_iota, one, zero))
        return jnp.concatenate(parts, axis=1)

    total = jnp.zeros((edge_count, proj_width), f32)
    for t in range(peers):
        slots = recv_ref[t, index_row:atom_row, :].astype(f32).astype(jnp.int32) + width // 2
        lane, row = slots % LANES, slots // LANES
        found = jnp.zeros(slots.shape, jnp.int32)
        for r in range(pieces):
            here = t * pieces + r
            table = jnp.where(
                upper,
                jnp.broadcast_to(send_ref[here : here + 1, :], slots.shape),
                jnp.broadcast_to(return_ref[here : here + 1, :], slots.shape),
            )
            got = jnp.take_along_axis(table, lane, axis=1, mode="promise_in_bounds")
            found = jnp.where(row == r, got, found)
        found = found.astype(f32)
        in_hot = one_hot(found[:pieces])
        gathered = matmul(expanded, in_hot)
        mixed = []
        for piece in range(pieces):
            coeffs = recv_ref[t, piece * basis_rows : (piece + 1) * basis_rows, :].astype(f32)
            part = None
            for k in range(basis_rows):
                term = (
                    gathered[k * proj_width : (k + 1) * proj_width, piece * LANES : (piece + 1) * LANES]
                    * coeffs[k : k + 1, :]
                )
                part = term if part is None else part + term
            mixed.append(part.astype(bf16))
        total = total + lax.dot_general(
            one_hot(found[pieces:]),
            jnp.concatenate(mixed, axis=1),
            (((1,), (1,)), ((), ())),
            preferred_element_type=f32,
        )

    base = ((edge.astype(f32) + activated.astype(f32)) * inv_root).astype(bf16)
    inner_one = silu(matmul(base, w_residual_ref[0])).astype(bf16)
    middle = ((base.astype(f32) + silu(matmul(inner_one, w_residual_ref[1]))) * inv_root).astype(bf16)
    inner_two = silu(matmul(middle, w_residual_ref[2])).astype(bf16)
    chain = (middle.astype(f32) + silu(matmul(inner_two, w_residual_ref[3]))) * inv_root
    update = silu(matmul(total.astype(bf16), w_up_ref[...]))
    edge_out = (chain + update).astype(bf16)
    edge_out_ref[...] = edge_out
    contrib = matmul(edge_out, w_atom_ref[...]).astype(bf16)
    atom_count = atom_ref.shape[0]
    target_hot = (
        lax.broadcasted_iota(jnp.int32, (atom_count, edge_count), 0) == target_ref[...]
    ).astype(f32).astype(bf16)
    atom_sum = matmul(target_hot, contrib)
    atom_out_ref[...] = (atom_ref[...].astype(f32) + silu(0.25 * atom_sum)).astype(bf16)


def local_blocks(
    peers,
    edge_state,
    atom_state,
    atom_sends,
    edge_source,
    edge_target,
    send_edges,
    triplet_in,
    triplet_out,
    triplet_valid,
    triplet_basis,
    return_edges,
    w_edge,
    w_source,
    w_down,
    w_bilinear,
    w_up,
    w_residual,
    w_atom,
):
    bf16 = jnp.bfloat16
    pieces = WIN // LANES
    rows = triplet_basis.shape[0] * pieces + 2 * pieces
    rows += atom_sends.shape[0] // peers * (atom_state.shape[1] // LANES)
    by_lanes = lambda array: array.reshape(-1, LANES)
    packed = pl.pallas_call(
        pack_kernel,
        out_shape=jax.ShapeDtypeStruct((peers, rows, LANES), bf16),
        name="pack",
    )(
        triplet_basis,
        by_lanes(triplet_valid),
        by_lanes(triplet_in),
        by_lanes(triplet_out),
        atom_state,
        atom_sends[None, :],
    )
    received = lax.all_to_all(packed, "graph", split_axis=0, concat_axis=0, tiled=True)
    return pl.pallas_call(
        main_kernel,
        out_shape=(
            jax.ShapeDtypeStruct(edge_state.shape, bf16),
            jax.ShapeDtypeStruct(atom_state.shape, bf16),
        ),
        compiler_params=pltpu.CompilerParams(vmem_limit_bytes=48 * 1024 * 1024),
        name="block",
    )(
        received,
        edge_state,
        atom_state,
        edge_source[None, :],
        edge_target[None, :],
        by_lanes(send_edges),
        by_lanes(return_edges),
        w_edge,
        w_source,
        w_down,
        w_bilinear,
        w_up,
        w_residual,
        w_atom,
    )


def bilinear_terms(inputs_x, coeffs, keeps, w_bilinear):
    expanded = matmul(inputs_x, w_bilinear)
    expanded = expanded.reshape(inputs_x.shape[0], coeffs.shape[0], -1)
    mixed = jnp.einsum("tkd,kt->td", expanded, coeffs.astype(jnp.float32))
    return mixed * keeps.astype(jnp.float32)[:, None]


def tile_sums(slot_rows, local_in, local_out, keeps, coeffs, w_bilinear):
    trip_count = slot_rows.shape[0]
    block_size = WIN
    block_count = trip_count // block_size
    basis_rows = coeffs.shape[0]
    block_iota = jnp.arange(block_size, dtype=jnp.int32)

    def one_block(operands):
        rows_blk, in_blk, out_blk, keep_blk, coef_blk = operands
        in_hot = ((in_blk % block_size)[:, None] == block_iota[None, :]).astype(jnp.bfloat16)
        inputs_x = matmul(in_hot, rows_blk).astype(jnp.bfloat16)
        mixed = bilinear_terms(inputs_x, coef_blk, keep_blk, w_bilinear)
        out_hot = (block_iota[:, None] == (out_blk % block_size)[None, :]).astype(jnp.float32)
        return jnp.dot(
            out_hot, mixed, precision=lax.Precision.HIGHEST, preferred_element_type=jnp.float32
        )

    shaped_coeffs = jnp.transpose(coeffs.reshape(basis_rows, block_count, block_size), (1, 0, 2))
    summed = lax.map(
        one_block,
        (
            slot_rows.reshape(block_count, block_size, -1),
            local_in.reshape(block_count, block_size),
            local_out.reshape(block_count, block_size),
            keeps.reshape(block_count, block_size),
            shaped_coeffs,
        ),
    )
    return summed.reshape(trip_count, -1).astype(jnp.bfloat16)


def on_tiles(
    edge_state,
    atom_state,
    atom_sends,
    edge_source,
    edge_target,
    send_edges,
    triplet_in,
    triplet_out,
    triplet_valid,
    triplet_basis,
    return_edges,
    w_edge,
    w_source,
    w_down,
    w_bilinear,
    w_up,
    w_residual,
    w_atom,
):
    edge_count = edge_state.shape[0]
    atom_count = atom_state.shape[0]
    arrived_atoms = lax.all_to_all(
        pick_rows(atom_sends, atom_state), "graph", split_axis=0, concat_axis=0, tiled=True
    )
    src_rows = pick_rows(edge_source, arrived_atoms)
    pre_act = matmul(edge_state, w_edge) + matmul(src_rows, w_source)
    activated = jax.nn.silu(pre_act).astype(jnp.bfloat16)
    projected = jax.nn.silu(matmul(activated, w_down)).astype(jnp.bfloat16)
    slot_rows = lax.all_to_all(
        pick_rows(send_edges, projected), "graph", split_axis=0, concat_axis=0, tiled=True
    )
    slot_sums = tile_sums(
        slot_rows, triplet_in, triplet_out, triplet_valid, triplet_basis, w_bilinear
    )
    returned = lax.all_to_all(slot_sums, "graph", split_axis=0, concat_axis=0, tiled=True)
    back_hot = (jnp.arange(edge_count, dtype=jnp.int32)[:, None] == return_edges[None, :]).astype(
        jnp.bfloat16
    )
    aggregate = matmul(back_hot, returned)
    update = jax.nn.silu(matmul(aggregate.astype(jnp.bfloat16), w_up))
    base = ((edge_state.astype(jnp.float32) + activated.astype(jnp.float32)) * inv_root).astype(
        jnp.bfloat16
    )
    inner_one = jax.nn.silu(matmul(base, w_residual[0])).astype(jnp.bfloat16)
    middle = (
        (base.astype(jnp.float32) + jax.nn.silu(matmul(inner_one, w_residual[1]))) * inv_root
    ).astype(jnp.bfloat16)
    inner_two = jax.nn.silu(matmul(middle, w_residual[2])).astype(jnp.bfloat16)
    chain = (middle.astype(jnp.float32) + jax.nn.silu(matmul(inner_two, w_residual[3]))) * inv_root
    edge_out = (chain + update).astype(jnp.bfloat16)
    contrib = matmul(edge_out, w_atom).astype(jnp.bfloat16)
    one_hot = (edge_target[None, :] == jnp.arange(atom_count, dtype=jnp.int32)[:, None]).astype(
        jnp.bfloat16
    )
    atom_sum = matmul(one_hot, contrib)
    atom_out = (atom_state.astype(jnp.float32) + jax.nn.silu(0.25 * atom_sum)).astype(jnp.bfloat16)
    return (edge_out, atom_out)


def on_device(*arguments):
    peers = lax.axis_size("graph")
    if arguments[5].shape[0] == peers * WIN:
        return local_blocks(peers, *arguments)
    return on_tiles(*arguments)


def solution(mesh):
    placed = (
        P(("groups", "graph"), None),
        P(("groups", "graph"), None),
        P(("groups", "graph")),
        P(("groups", "graph")),
        P(("groups", "graph")),
        P(("groups", "graph")),
        P(("groups", "graph")),
        P(("groups", "graph")),
        P(("groups", "graph")),
        P(None, ("groups", "graph")),
        P(("groups", "graph")),
        P(),
        P(),
        P(),
        P(),
        P(),
        P(),
        P(),
    )
    return jax.shard_map(
        on_device,
        mesh=mesh,
        in_specs=placed,
        out_specs=(P(("groups", "graph"), None), P(("groups", "graph"), None)),
        check_vma=False,
    )
```

```python
import functools

import jax
import jax.numpy as jnp
from jax import lax
from jax.experimental import pallas as pl
from jax.experimental.pallas import tpu as pltpu
from jax.sharding import PartitionSpec as P

WIN = 512
LANES = 128


inv_root = 0.7071067811865476


def matmul(left, right):
    return jnp.dot(left, right, preferred_element_type=jnp.float32)


def pick_rows(indices, table):
    chooser = (indices[:, None] == jnp.arange(table.shape[0], dtype=jnp.int32)[None, :]).astype(
        table.dtype
    )
    return matmul(chooser, table).astype(table.dtype)


def silu(v):
    return (0.5 * v) * (1.0 + jnp.tanh(0.5 * v))


def pack_kernel(basis_ref, valid_ref, in_ref, out_ref, atom_ref, sends_ref, send_ref):
    basis_rows = basis_ref.shape[0]
    peers = send_ref.shape[0]
    pieces = valid_ref.shape[0] // peers
    width = pieces * LANES
    atom_slots = sends_ref.shape[1]
    cap_a = atom_slots // peers
    chooser = (
        lax.broadcasted_iota(jnp.int32, (atom_ref.shape[0], atom_slots), 0) == sends_ref[...]
    ).astype(jnp.float32).astype(jnp.bfloat16)
    rows = lax.dot_general(
        chooser, atom_ref[...], (((0,), (0,)), ((), ())), preferred_element_type=jnp.float32
    ).astype(jnp.bfloat16)
    keeps = valid_ref[...].astype(jnp.float32)
    half = width // 2
    local_in = ((in_ref[...] % width) - half).astype(jnp.float32).astype(jnp.bfloat16)
    local_out = ((out_ref[...] % width) - half).astype(jnp.float32).astype(jnp.bfloat16)
    for peer in range(peers):
        parts = []
        for piece in range(pieces):
            row = peer * pieces + piece
            tile = basis_ref[:, row * LANES : (row + 1) * LANES].astype(jnp.float32)
            parts.append((tile * keeps[row : row + 1, :]).astype(jnp.bfloat16))
        parts.append(local_in[peer * pieces : (peer + 1) * pieces, :])
        parts.append(local_out[peer * pieces : (peer + 1) * pieces, :])
        for first in range(0, atom_ref.shape[1], LANES):
            parts.append(rows[peer * cap_a : (peer + 1) * cap_a, first : first + LANES])
        send_ref[peer] = jnp.concatenate(parts, axis=0)


def main_kernel(recv_ref, *refs):
    count = (len(refs) - 3) // 2
    far, (edge_out_ref, atom_out_ref) = refs[:count], refs[count : count + 2]
    near, sems = refs[count + 2 : -1], refs[-1]
    copies = [
        pltpu.make_async_copy(here, there, sems.at[at])
        for at, (here, there) in enumerate(zip(far, near))
    ]
    for copy in copies:
        copy.start()
    (
        edge_ref,
        w_edge_ref,
        source_ref,
        atom_ref,
        w_source_ref,
        w_down_t_ref,
        w_bilinear_ref,
        send_ref,
        return_ref,
        w_residual_ref,
        w_up_ref,
        w_atom_ref,
        target_ref,
    ) = near

    def ready(*ats):
        for at in ats:
            copies[at].wait()

    bf16, f32 = jnp.bfloat16, jnp.float32
    peers = recv_ref.shape[0]
    pieces = send_ref.shape[0] // peers
    width = pieces * LANES
    edge_count = edge_ref.shape[0]
    proj_width = w_down_t_ref.shape[0]
    basis_rows = w_bilinear_ref.shape[1] // proj_width
    index_row = basis_rows * pieces
    atom_row = index_row + 2 * pieces
    halves = atom_ref.shape[1] // LANES
    cap_a = (recv_ref.shape[1] - atom_row) // halves

    arrived = jnp.concatenate(
        [
            jnp.concatenate(
                [
                    recv_ref[s, atom_row + h * cap_a : atom_row + (h + 1) * cap_a, :]
                    for s in range(peers)
                ],
                axis=0,
            )
            for h in range(halves)
        ],
        axis=1,
    )
    ready(2)
    source_hot = (
        lax.broadcasted_iota(jnp.int32, (arrived.shape[0], edge_count), 0) == source_ref[...]
    ).astype(f32).astype(bf16)
    src_rows = lax.dot_general(
        source_hot, arrived, (((0,), (0,)), ((), ())), preferred_element_type=f32
    ).astype(bf16)
    ready(0, 1, 3, 4)
    edge = edge_ref[...]
    activated = silu(matmul(edge, w_edge_ref[...]) + matmul(src_rows, w_source_ref[...])).astype(bf16)
    ready(5, 6)
    projected = silu(
        lax.dot_general(
            activated, w_down_t_ref[...], (((1,), (1,)), ((), ())), preferred_element_type=f32
        )
    ).astype(bf16)
    expanded = lax.dot_general(
        w_bilinear_ref[...], projected, (((0,), (1,)), ((), ())), preferred_element_type=f32
    ).astype(bf16)

    ready(7, 8)
    edge_iota = lax.broadcasted_iota(jnp.int32, (edge_count, LANES), 0).astype(f32).astype(bf16)
    upper = lax.broadcasted_iota(jnp.int32, (2 * pieces, LANES), 0) < pieces
    one, zero = jnp.ones((), bf16), jnp.zeros((), bf16)

    def one_hot(rows):
        parts = []
        for piece in range(pieces):
            spread = jnp.broadcast_to(rows[piece : piece + 1, :], (edge_count, LANES)).astype(bf16)
            parts.append(jnp.where(spread == edge_iota, one, zero))
        return jnp.concatenate(parts, axis=1)

    total = jnp.zeros((edge_count, proj_width), f32)
    for t in range(peers):
        slots = recv_ref[t, index_row:atom_row, :].astype(f32).astype(jnp.int32) + width // 2
        lane, row = slots % LANES, slots // LANES
        found = jnp.zeros(slots.shape, jnp.int32)
        for r in range(pieces):
            here = t * pieces + r
            table = jnp.where(
                upper,
                jnp.broadcast_to(send_ref[here : here + 1, :], slots.shape),
                jnp.broadcast_to(return_ref[here : here + 1, :], slots.shape),
            )
            got = jnp.take_along_axis(table, lane, axis=1, mode="promise_in_bounds")
            found = jnp.where(row == r, got, found)
        found = found.astype(f32)
        in_hot = one_hot(found[:pieces])
        gathered = matmul(expanded, in_hot)
        mixed = []
        for piece in range(pieces):
            coeffs = recv_ref[t, piece * basis_rows : (piece + 1) * basis_rows, :].astype(f32)
            part = None
            for k in range(basis_rows):
                term = (
                    gathered[k * proj_width : (k + 1) * proj_width, piece * LANES : (piece + 1) * LANES]
                    * coeffs[k : k + 1, :]
                )
                part = term if part is None else part + term
            mixed.append(part.astype(bf16))
        total = total + lax.dot_general(
            one_hot(found[pieces:]),
            jnp.concatenate(mixed, axis=1),
            (((1,), (1,)), ((), ())),
            preferred_element_type=f32,
        )

    ready(9, 10, 11, 12)
    base = ((edge.astype(f32) + activated.astype(f32)) * inv_root).astype(bf16)
    inner_one = silu(matmul(base, w_residual_ref[0])).astype(bf16)
    middle = ((base.astype(f32) + silu(matmul(inner_one, w_residual_ref[1]))) * inv_root).astype(bf16)
    inner_two = silu(matmul(middle, w_residual_ref[2])).astype(bf16)
    chain = (middle.astype(f32) + silu(matmul(inner_two, w_residual_ref[3]))) * inv_root
    update = silu(matmul(total.astype(bf16), w_up_ref[...]))
    edge_out = (chain + update).astype(bf16)
    edge_out_ref[...] = edge_out
    contrib = matmul(edge_out, w_atom_ref[...]).astype(bf16)
    atom_count = atom_ref.shape[0]
    target_hot = (
        lax.broadcasted_iota(jnp.int32, (atom_count, edge_count), 0) == target_ref[...]
    ).astype(f32).astype(bf16)
    atom_sum = matmul(target_hot, contrib)
    atom_out_ref[...] = (atom_ref[...].astype(f32) + silu(0.25 * atom_sum)).astype(bf16)


def local_blocks(
    peers,
    edge_state,
    atom_state,
    atom_sends,
    edge_source,
    edge_target,
    send_edges,
    triplet_in,
    triplet_out,
    triplet_valid,
    triplet_basis,
    return_edges,
    w_edge,
    w_source,
    w_down,
    w_bilinear,
    w_up,
    w_residual,
    w_atom,
):
    bf16 = jnp.bfloat16
    pieces = WIN // LANES
    rows = triplet_basis.shape[0] * pieces + 2 * pieces
    rows += atom_sends.shape[0] // peers * (atom_state.shape[1] // LANES)
    by_lanes = lambda array: array.reshape(-1, LANES)
    packed = pl.pallas_call(
        pack_kernel,
        out_shape=jax.ShapeDtypeStruct((peers, rows, LANES), bf16),
        name="pack",
    )(
        triplet_basis,
        by_lanes(triplet_valid),
        by_lanes(triplet_in),
        by_lanes(triplet_out),
        atom_state,
        atom_sends[None, :],
    )
    received = lax.all_to_all(packed, "graph", split_axis=0, concat_axis=0, tiled=True)
    operands = (
        edge_state,
        w_edge,
        edge_source[None, :],
        atom_state,
        w_source,
        w_down.T,
        w_bilinear,
        by_lanes(send_edges),
        by_lanes(return_edges),
        w_residual,
        w_up,
        w_atom,
        edge_target[None, :],
    )
    like = lambda array: jax.ShapeDtypeStruct(array.shape, array.dtype)
    return pl.pallas_call(
        main_kernel,
        in_specs=[pl.BlockSpec(memory_space=pltpu.VMEM)]
        + [pl.BlockSpec(memory_space=pltpu.HBM)] * len(operands),
        out_shape=(like(edge_state), like(atom_state)),
        scratch_shapes=[pltpu.VMEM(array.shape, array.dtype) for array in operands]
        + [pltpu.SemaphoreType.DMA((len(operands),))],
        compiler_params=pltpu.CompilerParams(vmem_limit_bytes=32 * 1024 * 1024),
        name="block",
    )(received, *(pltpu.with_memory_space_constraint(array, pltpu.HBM) for array in operands))


def bilinear_terms(inputs_x, coeffs, keeps, w_bilinear):
    expanded = matmul(inputs_x, w_bilinear)
    expanded = expanded.reshape(inputs_x.shape[0], coeffs.shape[0], -1)
    mixed = jnp.einsum("tkd,kt->td", expanded, coeffs.astype(jnp.float32))
    return mixed * keeps.astype(jnp.float32)[:, None]


def tile_sums(slot_rows, local_in, local_out, keeps, coeffs, w_bilinear):
    trip_count = slot_rows.shape[0]
    block_size = WIN
    block_count = trip_count // block_size
    basis_rows = coeffs.shape[0]
    block_iota = jnp.arange(block_size, dtype=jnp.int32)

    def one_block(operands):
        rows_blk, in_blk, out_blk, keep_blk, coef_blk = operands
        in_hot = ((in_blk % block_size)[:, None] == block_iota[None, :]).astype(jnp.bfloat16)
        inputs_x = matmul(in_hot, rows_blk).astype(jnp.bfloat16)
        mixed = bilinear_terms(inputs_x, coef_blk, keep_blk, w_bilinear)
        out_hot = (block_iota[:, None] == (out_blk % block_size)[None, :]).astype(jnp.float32)
        return jnp.dot(
            out_hot, mixed, precision=lax.Precision.HIGHEST, preferred_element_type=jnp.float32
        )

    shaped_coeffs = jnp.transpose(coeffs.reshape(basis_rows, block_count, block_size), (1, 0, 2))
    summed = lax.map(
        one_block,
        (
            slot_rows.reshape(block_count, block_size, -1),
            local_in.reshape(block_count, block_size),
            local_out.reshape(block_count, block_size),
            keeps.reshape(block_count, block_size),
            shaped_coeffs,
        ),
    )
    return summed.reshape(trip_count, -1).astype(jnp.bfloat16)


def on_tiles(
    edge_state,
    atom_state,
    atom_sends,
    edge_source,
    edge_target,
    send_edges,
    triplet_in,
    triplet_out,
    triplet_valid,
    triplet_basis,
    return_edges,
    w_edge,
    w_source,
    w_down,
    w_bilinear,
    w_up,
    w_residual,
    w_atom,
):
    edge_count = edge_state.shape[0]
    atom_count = atom_state.shape[0]
    arrived_atoms = lax.all_to_all(
        pick_rows(atom_sends, atom_state), "graph", split_axis=0, concat_axis=0, tiled=True
    )
    src_rows = pick_rows(edge_source, arrived_atoms)
    pre_act = matmul(edge_state, w_edge) + matmul(src_rows, w_source)
    activated = jax.nn.silu(pre_act).astype(jnp.bfloat16)
    projected = jax.nn.silu(matmul(activated, w_down)).astype(jnp.bfloat16)
    slot_rows = lax.all_to_all(
        pick_rows(send_edges, projected), "graph", split_axis=0, concat_axis=0, tiled=True
    )
    slot_sums = tile_sums(
        slot_rows, triplet_in, triplet_out, triplet_valid, triplet_basis, w_bilinear
    )
    returned = lax.all_to_all(slot_sums, "graph", split_axis=0, concat_axis=0, tiled=True)
    back_hot = (jnp.arange(edge_count, dtype=jnp.int32)[:, None] == return_edges[None, :]).astype(
        jnp.bfloat16
    )
    aggregate = matmul(back_hot, returned)
    update = jax.nn.silu(matmul(aggregate.astype(jnp.bfloat16), w_up))
    base = ((edge_state.astype(jnp.float32) + activated.astype(jnp.float32)) * inv_root).astype(
        jnp.bfloat16
    )
    inner_one = jax.nn.silu(matmul(base, w_residual[0])).astype(jnp.bfloat16)
    middle = (
        (base.astype(jnp.float32) + jax.nn.silu(matmul(inner_one, w_residual[1]))) * inv_root
    ).astype(jnp.bfloat16)
    inner_two = jax.nn.silu(matmul(middle, w_residual[2])).astype(jnp.bfloat16)
    chain = (middle.astype(jnp.float32) + jax.nn.silu(matmul(inner_two, w_residual[3]))) * inv_root
    edge_out = (chain + update).astype(jnp.bfloat16)
    contrib = matmul(edge_out, w_atom).astype(jnp.bfloat16)
    one_hot = (edge_target[None, :] == jnp.arange(atom_count, dtype=jnp.int32)[:, None]).astype(
        jnp.bfloat16
    )
    atom_sum = matmul(one_hot, contrib)
    atom_out = (atom_state.astype(jnp.float32) + jax.nn.silu(0.25 * atom_sum)).astype(jnp.bfloat16)
    return (edge_out, atom_out)


def on_device(*arguments):
    peers = lax.axis_size("graph")
    if arguments[5].shape[0] == peers * WIN:
        return local_blocks(peers, *arguments)
    return on_tiles(*arguments)


def solution(mesh):
    placed = (
        P(("groups", "graph"), None),
        P(("groups", "graph"), None),
        P(("groups", "graph")),
        P(("groups", "graph")),
        P(("groups", "graph")),
        P(("groups", "graph")),
        P(("groups", "graph")),
        P(("groups", "graph")),
        P(("groups", "graph")),
        P(None, ("groups", "graph")),
        P(("groups", "graph")),
        P(),
        P(),
        P(),
        P(),
        P(),
        P(),
        P(),
    )
    return jax.shard_map(
        on_device,
        mesh=mesh,
        in_specs=placed,
        out_specs=(P(("groups", "graph"), None), P(("groups", "graph"), None)),
        check_vma=False,
    )
```

```python
import jax
import jax.numpy as jnp
from jax import lax
from jax.experimental import pallas as pl
from jax.experimental.pallas import tpu as pltpu
from jax.sharding import PartitionSpec as P

WIN = 512
LANES = 128


inv_root = 0.7071067811865476


def matmul(left, right):
    return jnp.dot(left, right, preferred_element_type=jnp.float32)


def pick_rows(indices, table):
    chooser = (indices[:, None] == jnp.arange(table.shape[0], dtype=jnp.int32)[None, :]).astype(
        table.dtype
    )
    return matmul(chooser, table).astype(table.dtype)


def silu(v):
    return (0.5 * v) * (1.0 + jnp.tanh(0.5 * v))


def pack_kernel(basis_ref, valid_ref, in_ref, out_ref, atom_ref, sends_ref, send_ref):
    basis_rows = basis_ref.shape[0]
    peers = send_ref.shape[0]
    pieces = valid_ref.shape[0] // peers
    width = pieces * LANES
    atom_slots = sends_ref.shape[1]
    cap_a = atom_slots // peers
    chooser = (
        lax.broadcasted_iota(jnp.int32, (atom_ref.shape[0], atom_slots), 0) == sends_ref[...]
    ).astype(jnp.float32).astype(jnp.bfloat16)
    rows = lax.dot_general(
        chooser, atom_ref[...], (((0,), (0,)), ((), ())), preferred_element_type=jnp.float32
    ).astype(jnp.bfloat16)
    keeps = valid_ref[...].astype(jnp.float32)
    half = width // 2
    local_in = ((in_ref[...] % width) - half).astype(jnp.float32).astype(jnp.bfloat16)
    local_out = ((out_ref[...] % width) - half).astype(jnp.float32).astype(jnp.bfloat16)
    for peer in range(peers):
        parts = []
        for piece in range(pieces):
            row = peer * pieces + piece
            tile = basis_ref[:, row * LANES : (row + 1) * LANES].astype(jnp.float32)
            parts.append((tile * keeps[row : row + 1, :]).astype(jnp.bfloat16))
        parts.append(local_in[peer * pieces : (peer + 1) * pieces, :])
        parts.append(local_out[peer * pieces : (peer + 1) * pieces, :])
        for first in range(0, atom_ref.shape[1], LANES):
            parts.append(rows[peer * cap_a : (peer + 1) * cap_a, first : first + LANES])
        send_ref[peer] = jnp.concatenate(parts, axis=0)


def ahead_kernel(
    edge_far,
    w_edge_far,
    source_far,
    w_bilinear_far,
    w_source_far,
    w_down_t_far,
    edge_ref,
    pre_ref,
    source_hot_ref,
    w_bilinear_t_ref,
    w_source_ref,
    w_down_t_ref,
    w_edge_ref,
    source_ref,
    w_bilinear_ref,
    sems,
):
    copies = [
        pltpu.make_async_copy(here, there, sems.at[at])
        for at, (here, there) in enumerate(
            (
                (edge_far, edge_ref),
                (w_edge_far, w_edge_ref),
                (source_far, source_ref),
                (w_bilinear_far, w_bilinear_ref),
                (w_source_far, w_source_ref),
                (w_down_t_far, w_down_t_ref),
            )
        )
    ]
    for copy in copies:
        copy.start()
    for copy in copies:
        copy.wait()
    pre_ref[...] = matmul(edge_ref[...], w_edge_ref[...])
    w_bilinear_t_ref[...] = w_bilinear_ref[...].T
    hot = lax.broadcasted_iota(jnp.int32, source_hot_ref.shape[::-1], 0) == source_ref[...]
    source_hot_ref[...] = hot.astype(jnp.float32).T.astype(jnp.bfloat16)


def main_kernel(
    recv_ref,
    edge_ref,
    pre_ref,
    source_hot_ref,
    w_bilinear_t_ref,
    w_source_ref,
    w_down_t_ref,
    *refs,
):
    count = (len(refs) - 3) // 2
    far, (edge_out_ref, atom_out_ref) = refs[:count], refs[count : count + 2]
    near, sems = refs[count + 2 : -1], refs[-1]
    copies = [
        pltpu.make_async_copy(here, there, sems.at[at])
        for at, (here, there) in enumerate(zip(far, near))
    ]
    for copy in copies:
        copy.start()
    send_ref, return_ref, w_residual_ref, w_up_ref, w_atom_ref, target_ref, atom_ref = near

    def ready(*ats):
        for at in ats:
            copies[at].wait()

    bf16, f32 = jnp.bfloat16, jnp.float32
    peers = recv_ref.shape[0]
    pieces = send_ref.shape[0] // peers
    width = pieces * LANES
    edge_count = edge_ref.shape[0]
    proj_width = w_down_t_ref.shape[0]
    basis_rows = w_bilinear_t_ref.shape[0] // proj_width
    index_row = basis_rows * pieces
    atom_row = index_row + 2 * pieces
    halves = atom_out_ref.shape[1] // LANES
    cap_a = (recv_ref.shape[1] - atom_row) // halves

    arrived = jnp.concatenate(
        [
            jnp.concatenate(
                [
                    recv_ref[s, atom_row + h * cap_a : atom_row + (h + 1) * cap_a, :]
                    for s in range(peers)
                ],
                axis=0,
            )
            for h in range(halves)
        ],
        axis=1,
    )
    src_rows = matmul(source_hot_ref[...], arrived).astype(bf16)
    edge = edge_ref[...]
    activated = silu(pre_ref[...] + matmul(src_rows, w_source_ref[...])).astype(bf16)
    projected = silu(
        lax.dot_general(
            activated, w_down_t_ref[...], (((1,), (1,)), ((), ())), preferred_element_type=f32
        )
    ).astype(bf16)
    expanded = lax.dot_general(
        w_bilinear_t_ref[...], projected, (((1,), (1,)), ((), ())), preferred_element_type=f32
    ).astype(bf16)

    ready(0, 1)
    edge_iota = lax.broadcasted_iota(jnp.int32, (edge_count, LANES), 0).astype(f32).astype(bf16)
    upper = lax.broadcasted_iota(jnp.int32, (2 * pieces, LANES), 0) < pieces
    one, zero = jnp.ones((), bf16), jnp.zeros((), bf16)

    def one_hot(rows):
        parts = []
        for piece in range(pieces):
            spread = jnp.broadcast_to(rows[piece : piece + 1, :], (edge_count, LANES)).astype(bf16)
            parts.append(jnp.where(spread == edge_iota, one, zero))
        return jnp.concatenate(parts, axis=1)

    total = jnp.zeros((edge_count, proj_width), f32)
    for t in range(peers):
        slots = recv_ref[t, index_row:atom_row, :].astype(f32).astype(jnp.int32) + width // 2
        lane, row = slots % LANES, slots // LANES
        found = jnp.zeros(slots.shape, jnp.int32)
        for r in range(pieces):
            here = t * pieces + r
            table = jnp.where(
                upper,
                jnp.broadcast_to(send_ref[here : here + 1, :], slots.shape),
                jnp.broadcast_to(return_ref[here : here + 1, :], slots.shape),
            )
            got = jnp.take_along_axis(table, lane, axis=1, mode="promise_in_bounds")
            found = jnp.where(row == r, got, found)
        found = found.astype(f32)
        in_hot = one_hot(found[:pieces])
        gathered = matmul(expanded, in_hot)
        mixed = []
        for piece in range(pieces):
            coeffs = recv_ref[t, piece * basis_rows : (piece + 1) * basis_rows, :].astype(f32)
            part = None
            for k in range(basis_rows):
                term = (
                    gathered[k * proj_width : (k + 1) * proj_width, piece * LANES : (piece + 1) * LANES]
                    * coeffs[k : k + 1, :]
                )
                part = term if part is None else part + term
            mixed.append(part.astype(bf16))
        total = total + lax.dot_general(
            one_hot(found[pieces:]),
            jnp.concatenate(mixed, axis=1),
            (((1,), (1,)), ((), ())),
            preferred_element_type=f32,
        )

    ready(2, 3, 4, 5, 6)
    base = ((edge.astype(f32) + activated.astype(f32)) * inv_root).astype(bf16)
    inner_one = silu(matmul(base, w_residual_ref[0])).astype(bf16)
    middle = ((base.astype(f32) + silu(matmul(inner_one, w_residual_ref[1]))) * inv_root).astype(bf16)
    inner_two = silu(matmul(middle, w_residual_ref[2])).astype(bf16)
    chain = (middle.astype(f32) + silu(matmul(inner_two, w_residual_ref[3]))) * inv_root
    update = silu(matmul(total.astype(bf16), w_up_ref[...]))
    edge_out = (chain + update).astype(bf16)
    edge_out_ref[...] = edge_out
    contrib = matmul(edge_out, w_atom_ref[...]).astype(bf16)
    atom_count = atom_ref.shape[0]
    target_hot = (
        lax.broadcasted_iota(jnp.int32, (atom_count, edge_count), 0) == target_ref[...]
    ).astype(f32).astype(bf16)
    atom_sum = matmul(target_hot, contrib)
    atom_out_ref[...] = (atom_ref[...].astype(f32) + silu(0.25 * atom_sum)).astype(bf16)


def local_blocks(
    peers,
    edge_state,
    atom_state,
    atom_sends,
    edge_source,
    edge_target,
    send_edges,
    triplet_in,
    triplet_out,
    triplet_valid,
    triplet_basis,
    return_edges,
    w_edge,
    w_source,
    w_down,
    w_bilinear,
    w_up,
    w_residual,
    w_atom,
):
    bf16 = jnp.bfloat16
    pieces = WIN // LANES
    rows = triplet_basis.shape[0] * pieces + 2 * pieces
    rows += atom_sends.shape[0] // peers * (atom_state.shape[1] // LANES)
    by_lanes = lambda array: array.reshape(-1, LANES)
    packed = pl.pallas_call(
        pack_kernel,
        out_shape=jax.ShapeDtypeStruct((peers, rows, LANES), bf16),
        name="pack",
    )(
        triplet_basis,
        by_lanes(triplet_valid),
        by_lanes(triplet_in),
        by_lanes(triplet_out),
        atom_state,
        atom_sends[None, :],
    )
    received = lax.all_to_all(packed, "graph", split_axis=0, concat_axis=0, tiled=True)
    like = lambda array: jax.ShapeDtypeStruct(array.shape, array.dtype)
    stay = lambda arrays: [pltpu.with_memory_space_constraint(one, pltpu.HBM) for one in arrays]
    near, far = pl.BlockSpec(memory_space=pltpu.VMEM), pl.BlockSpec(memory_space=pltpu.HBM)
    source, w_down_t = edge_source[None, :], w_down.T
    early = pl.pallas_call(
        ahead_kernel,
        in_specs=[far] * 6,
        out_specs=[near] * 6,
        out_shape=(
            like(edge_state),
            jax.ShapeDtypeStruct((edge_state.shape[0], w_edge.shape[1]), jnp.float32),
            jax.ShapeDtypeStruct((edge_state.shape[0], atom_sends.shape[0]), bf16),
            jax.ShapeDtypeStruct(w_bilinear.shape[::-1], bf16),
            like(w_source),
            like(w_down_t),
        ),
        scratch_shapes=[
            pltpu.VMEM(array.shape, array.dtype) for array in (w_edge, source, w_bilinear)
        ]
        + [pltpu.SemaphoreType.DMA((6,))],
        compiler_params=pltpu.CompilerParams(vmem_limit_bytes=8 * 1024 * 1024),
        name="ahead",
    )(*stay((edge_state, w_edge, source, w_bilinear, w_source, w_down_t)))
    late = (
        by_lanes(send_edges),
        by_lanes(return_edges),
        w_residual,
        w_up,
        w_atom,
        edge_target[None, :],
        atom_state,
    )
    return pl.pallas_call(
        main_kernel,
        in_specs=[near] * 7 + [far] * len(late),
        out_shape=(like(edge_state), like(atom_state)),
        scratch_shapes=[pltpu.VMEM(array.shape, array.dtype) for array in late]
        + [pltpu.SemaphoreType.DMA((len(late),))],
        compiler_params=pltpu.CompilerParams(vmem_limit_bytes=32 * 1024 * 1024),
        name="block",
    )(received, *early, *stay(late))


def bilinear_terms(inputs_x, coeffs, keeps, w_bilinear):
    expanded = matmul(inputs_x, w_bilinear)
    expanded = expanded.reshape(inputs_x.shape[0], coeffs.shape[0], -1)
    mixed = jnp.einsum("tkd,kt->td", expanded, coeffs.astype(jnp.float32))
    return mixed * keeps.astype(jnp.float32)[:, None]


def tile_sums(slot_rows, local_in, local_out, keeps, coeffs, w_bilinear):
    trip_count = slot_rows.shape[0]
    block_size = WIN
    block_count = trip_count // block_size
    basis_rows = coeffs.shape[0]
    block_iota = jnp.arange(block_size, dtype=jnp.int32)

    def one_block(operands):
        rows_blk, in_blk, out_blk, keep_blk, coef_blk = operands
        in_hot = ((in_blk % block_size)[:, None] == block_iota[None, :]).astype(jnp.bfloat16)
        inputs_x = matmul(in_hot, rows_blk).astype(jnp.bfloat16)
        mixed = bilinear_terms(inputs_x, coef_blk, keep_blk, w_bilinear)
        out_hot = (block_iota[:, None] == (out_blk % block_size)[None, :]).astype(jnp.float32)
        return jnp.dot(
            out_hot, mixed, precision=lax.Precision.HIGHEST, preferred_element_type=jnp.float32
        )

    shaped_coeffs = jnp.transpose(coeffs.reshape(basis_rows, block_count, block_size), (1, 0, 2))
    summed = lax.map(
        one_block,
        (
            slot_rows.reshape(block_count, block_size, -1),
            local_in.reshape(block_count, block_size),
            local_out.reshape(block_count, block_size),
            keeps.reshape(block_count, block_size),
            shaped_coeffs,
        ),
    )
    return summed.reshape(trip_count, -1).astype(jnp.bfloat16)


def on_tiles(
    edge_state,
    atom_state,
    atom_sends,
    edge_source,
    edge_target,
    send_edges,
    triplet_in,
    triplet_out,
    triplet_valid,
    triplet_basis,
    return_edges,
    w_edge,
    w_source,
    w_down,
    w_bilinear,
    w_up,
    w_residual,
    w_atom,
):
    edge_count = edge_state.shape[0]
    atom_count = atom_state.shape[0]
    arrived_atoms = lax.all_to_all(
        pick_rows(atom_sends, atom_state), "graph", split_axis=0, concat_axis=0, tiled=True
    )
    src_rows = pick_rows(edge_source, arrived_atoms)
    pre_act = matmul(edge_state, w_edge) + matmul(src_rows, w_source)
    activated = jax.nn.silu(pre_act).astype(jnp.bfloat16)
    projected = jax.nn.silu(matmul(activated, w_down)).astype(jnp.bfloat16)
    slot_rows = lax.all_to_all(
        pick_rows(send_edges, projected), "graph", split_axis=0, concat_axis=0, tiled=True
    )
    slot_sums = tile_sums(
        slot_rows, triplet_in, triplet_out, triplet_valid, triplet_basis, w_bilinear
    )
    returned = lax.all_to_all(slot_sums, "graph", split_axis=0, concat_axis=0, tiled=True)
    back_hot = (jnp.arange(edge_count, dtype=jnp.int32)[:, None] == return_edges[None, :]).astype(
        jnp.bfloat16
    )
    aggregate = matmul(back_hot, returned)
    update = jax.nn.silu(matmul(aggregate.astype(jnp.bfloat16), w_up))
    base = ((edge_state.astype(jnp.float32) + activated.astype(jnp.float32)) * inv_root).astype(
        jnp.bfloat16
    )
    inner_one = jax.nn.silu(matmul(base, w_residual[0])).astype(jnp.bfloat16)
    middle = (
        (base.astype(jnp.float32) + jax.nn.silu(matmul(inner_one, w_residual[1]))) * inv_root
    ).astype(jnp.bfloat16)
    inner_two = jax.nn.silu(matmul(middle, w_residual[2])).astype(jnp.bfloat16)
    chain = (middle.astype(jnp.float32) + jax.nn.silu(matmul(inner_two, w_residual[3]))) * inv_root
    edge_out = (chain + update).astype(jnp.bfloat16)
    contrib = matmul(edge_out, w_atom).astype(jnp.bfloat16)
    one_hot = (edge_target[None, :] == jnp.arange(atom_count, dtype=jnp.int32)[:, None]).astype(
        jnp.bfloat16
    )
    atom_sum = matmul(one_hot, contrib)
    atom_out = (atom_state.astype(jnp.float32) + jax.nn.silu(0.25 * atom_sum)).astype(jnp.bfloat16)
    return (edge_out, atom_out)


def on_device(*arguments):
    peers = lax.axis_size("graph")
    if arguments[5].shape[0] == peers * WIN:
        return local_blocks(peers, *arguments)
    return on_tiles(*arguments)


def solution(mesh):
    placed = (
        P(("groups", "graph"), None),
        P(("groups", "graph"), None),
        P(("groups", "graph")),
        P(("groups", "graph")),
        P(("groups", "graph")),
        P(("groups", "graph")),
        P(("groups", "graph")),
        P(("groups", "graph")),
        P(("groups", "graph")),
        P(None, ("groups", "graph")),
        P(("groups", "graph")),
        P(),
        P(),
        P(),
        P(),
        P(),
        P(),
        P(),
    )
    return jax.shard_map(
        on_device,
        mesh=mesh,
        in_specs=placed,
        out_specs=(P(("groups", "graph"), None), P(("groups", "graph"), None)),
        check_vma=False,
    )
```

```python
import jax
import jax.numpy as jnp
from jax import lax
from jax.experimental import pallas as pl
from jax.experimental.pallas import tpu as pltpu
from jax.sharding import PartitionSpec as P

WIN = 512
LANES = 128


inv_root = 0.7071067811865476


def matmul(left, right):
    return jnp.dot(left, right, preferred_element_type=jnp.float32)


def pick_rows(indices, table):
    chooser = (indices[:, None] == jnp.arange(table.shape[0], dtype=jnp.int32)[None, :]).astype(
        table.dtype
    )
    return matmul(chooser, table).astype(table.dtype)


def silu(v):
    return (0.5 * v) * (1.0 + jnp.tanh(0.5 * v))


def pack_kernel(basis_ref, valid_ref, in_ref, out_ref, atom_ref, sends_ref, send_ref):
    basis_rows = basis_ref.shape[0]
    peers = send_ref.shape[0]
    pieces = valid_ref.shape[0] // peers
    width = pieces * LANES
    atom_slots = sends_ref.shape[1]
    cap_a = atom_slots // peers
    chooser = (
        lax.broadcasted_iota(jnp.int32, (atom_ref.shape[0], atom_slots), 0) == sends_ref[...]
    ).astype(jnp.float32).astype(jnp.bfloat16)
    rows = lax.dot_general(
        chooser, atom_ref[...], (((0,), (0,)), ((), ())), preferred_element_type=jnp.float32
    ).astype(jnp.bfloat16)
    keeps = valid_ref[...].astype(jnp.float32)
    half = width // 2
    local_in = ((in_ref[...] % width) - half).astype(jnp.float32).astype(jnp.bfloat16)
    local_out = ((out_ref[...] % width) - half).astype(jnp.float32).astype(jnp.bfloat16)
    for peer in range(peers):
        parts = []
        for piece in range(pieces):
            row = peer * pieces + piece
            tile = basis_ref[:, row * LANES : (row + 1) * LANES].astype(jnp.float32)
            parts.append((tile * keeps[row : row + 1, :]).astype(jnp.bfloat16))
        parts.append(local_in[peer * pieces : (peer + 1) * pieces, :])
        parts.append(local_out[peer * pieces : (peer + 1) * pieces, :])
        for first in range(0, atom_ref.shape[1], LANES):
            parts.append(rows[peer * cap_a : (peer + 1) * cap_a, first : first + LANES])
        send_ref[peer] = jnp.concatenate(parts, axis=0)


def ahead_kernel(
    edge_far,
    w_edge_far,
    source_far,
    w_bilinear_far,
    target_far,
    atom_far,
    w_source_far,
    w_down_t_far,
    send_far,
    return_far,
    w_up_far,
    w_residual_far,
    edge_ref,
    pre_ref,
    source_hot_ref,
    w_mix_ref,
    w_source_ref,
    w_narrow_ref,
    index_ref,
    w_residual_ref,
    atom_rows_ref,
    w_edge_ref,
    source_ref,
    w_bilinear_ref,
    target_ref,
    sems,
):
    f32, bf16 = jnp.float32, jnp.bfloat16
    slots, narrow, atoms = send_far.shape[0], w_down_t_far.shape[0], atom_far.shape[0]
    copies = [
        pltpu.make_async_copy(here, there, sems.at[at])
        for at, (here, there) in enumerate(
            (
                (edge_far, edge_ref),
                (w_edge_far, w_edge_ref),
                (source_far, source_ref),
                (w_bilinear_far, w_bilinear_ref),
                (target_far, target_ref),
                (atom_far, atom_rows_ref.at[pl.ds(0, atoms), :]),
                (w_source_far, w_source_ref),
                (w_down_t_far, w_narrow_ref.at[pl.ds(0, narrow), :]),
                (w_up_far, w_narrow_ref.at[pl.ds(narrow, narrow), :]),
                (send_far, index_ref.at[pl.ds(0, slots), :]),
                (return_far, index_ref.at[pl.ds(slots, slots), :]),
                (w_residual_far.at[pl.ds(0, w_residual_ref.shape[0])], w_residual_ref),
            )
        )
    ]
    for copy in copies:
        copy.start()
    for copy in copies[:5]:
        copy.wait()
    pre_ref[...] = matmul(edge_ref[...], w_edge_ref[...])
    for first in range(0, w_mix_ref.shape[1], 2 * narrow):
        w_mix_ref[:, first : first + 2 * narrow] = jnp.concatenate(
            [
                w_bilinear_ref[:, at : at + narrow].astype(f32).T
                for at in (first, first + narrow)
            ],
            axis=1,
        ).astype(bf16)
    hot = lax.broadcasted_iota(jnp.int32, source_hot_ref.shape[::-1], 0) == source_ref[...]
    source_hot_ref[...] = hot.astype(f32).T.astype(bf16)
    hot = lax.broadcasted_iota(jnp.int32, (atoms, target_ref.shape[1]), 0) == target_ref[...]
    atom_rows_ref[atoms:, :] = hot.astype(f32).astype(bf16)
    for copy in copies[5:]:
        copy.wait()


def main_kernel(
    recv_ref,
    edge_ref,
    pre_ref,
    source_hot_ref,
    w_mix_ref,
    w_source_ref,
    w_narrow_ref,
    index_ref,
    w_residual_ref,
    atom_rows_ref,
    w_last_far,
    w_atom_far,
    edge_out_ref,
    atom_out_ref,
    w_last_ref,
    w_atom_ref,
    sems,
):
    copies = [
        pltpu.make_async_copy(w_last_far.at[w_residual_ref.shape[0]], w_last_ref, sems.at[0]),
        pltpu.make_async_copy(w_atom_far, w_atom_ref, sems.at[1]),
    ]
    for copy in copies:
        copy.start()
    bf16, f32 = jnp.bfloat16, jnp.float32
    peers = recv_ref.shape[0]
    slot_rows = index_ref.shape[0] // 2
    pieces = slot_rows // peers
    width = pieces * LANES
    edge_count = edge_ref.shape[0]
    proj_width = w_mix_ref.shape[0]
    atom_count = atom_out_ref.shape[0]
    basis_rows = w_mix_ref.shape[1] // proj_width
    index_row = basis_rows * pieces
    atom_row = index_row + 2 * pieces
    halves = atom_out_ref.shape[1] // LANES
    cap_a = (recv_ref.shape[1] - atom_row) // halves

    arrived = jnp.concatenate(
        [
            jnp.concatenate(
                [
                    recv_ref[s, atom_row + h * cap_a : atom_row + (h + 1) * cap_a, :]
                    for s in range(peers)
                ],
                axis=0,
            )
            for h in range(halves)
        ],
        axis=1,
    )
    src_rows = matmul(source_hot_ref[...], arrived).astype(bf16)
    edge = edge_ref[...]
    activated = silu(pre_ref[...] + matmul(src_rows, w_source_ref[...])).astype(bf16)
    projected = silu(
        lax.dot_general(
            w_narrow_ref[:proj_width, :], activated, (((1,), (1,)), ((), ())), preferred_element_type=f32
        )
    ).astype(bf16)
    w_mix = w_mix_ref[...]

    edge_iota = lax.broadcasted_iota(jnp.int32, (edge_count, LANES), 0).astype(f32).astype(bf16)
    packed = 16
    upper = lax.broadcasted_iota(jnp.int32, (2 * pieces, LANES), 0) < pieces
    one, zero = jnp.ones((), bf16), jnp.zeros((), bf16)

    def one_hot(rows):
        parts = []
        for piece in range(pieces):
            spread = jnp.broadcast_to(rows[piece : piece + 1, :], (packed, LANES)).astype(bf16)
            spread = jnp.concatenate([spread] * (edge_count // packed), axis=0)
            parts.append(jnp.where(spread == edge_iota, one, zero))
        return jnp.concatenate(parts, axis=1)

    middle = ((edge.astype(f32) + activated.astype(f32)) * inv_root).astype(bf16)
    inner, stage = None, 0
    total = jnp.zeros((edge_count, proj_width), f32)
    for t in range(peers):
        slots = recv_ref[t, index_row:atom_row, :].astype(f32).astype(jnp.int32) + width // 2
        lane, row = slots % LANES, slots // LANES
        found = jnp.zeros(slots.shape, jnp.int32)
        for r in range(pieces):
            here = t * pieces + r
            table = jnp.where(
                upper,
                jnp.broadcast_to(index_ref[here : here + 1, :], slots.shape),
                jnp.broadcast_to(
                    index_ref[slot_rows + here : slot_rows + here + 1, :], slots.shape
                ),
            )
            got = jnp.take_along_axis(table, lane, axis=1, mode="promise_in_bounds")
            found = jnp.where(row == r, got, found)
        found = found.astype(f32)
        in_hot = one_hot(found[:pieces])
        rows = matmul(projected, in_hot).astype(bf16)
        coeffs = jnp.concatenate(
            [
                recv_ref[t, piece * basis_rows : (piece + 1) * basis_rows, :]
                for piece in range(pieces)
            ],
            axis=1,
        )
        terms = jnp.concatenate(
            [rows * coeffs[k : k + 1, :] for k in range(basis_rows)], axis=0
        )
        mixed = matmul(w_mix, terms).astype(bf16)
        total = total + lax.dot_general(
            one_hot(found[pieces:]), mixed, (((1,), (1,)), ((), ())), preferred_element_type=f32
        )
        if (t + 1) * w_residual_ref.shape[0] // peers > stage:
            grown = silu(matmul(middle if stage % 2 == 0 else inner, w_residual_ref[stage]))
            if stage % 2 == 0:
                inner = grown.astype(bf16)
            else:
                middle = ((middle.astype(f32) + grown) * inv_root).astype(bf16)
            stage += 1
    for copy in copies:
        copy.wait()
    chain = (middle.astype(f32) + silu(matmul(inner, w_last_ref[...]))) * inv_root
    update = silu(matmul(total.astype(bf16), w_narrow_ref[proj_width:, :]))
    edge_out = (chain + update).astype(bf16)
    edge_out_ref[...] = edge_out
    contrib = matmul(edge_out, w_atom_ref[...]).astype(bf16)
    atom_sum = matmul(atom_rows_ref[atom_count:, :], contrib)
    atom_out_ref[...] = (
        atom_rows_ref[:atom_count, :].astype(f32) + silu(0.25 * atom_sum)
    ).astype(bf16)


def local_blocks(
    peers,
    edge_state,
    atom_state,
    atom_sends,
    edge_source,
    edge_target,
    send_edges,
    triplet_in,
    triplet_out,
    triplet_valid,
    triplet_basis,
    return_edges,
    w_edge,
    w_source,
    w_down,
    w_bilinear,
    w_up,
    w_residual,
    w_atom,
):
    bf16 = jnp.bfloat16
    pieces = WIN // LANES
    rows = triplet_basis.shape[0] * pieces + 2 * pieces
    rows += atom_sends.shape[0] // peers * (atom_state.shape[1] // LANES)
    by_lanes = lambda array: array.reshape(-1, LANES)
    packed = pl.pallas_call(
        pack_kernel,
        out_shape=jax.ShapeDtypeStruct((peers, rows, LANES), bf16),
        name="pack",
    )(
        triplet_basis,
        by_lanes(triplet_valid),
        by_lanes(triplet_in),
        by_lanes(triplet_out),
        atom_state,
        atom_sends[None, :],
    )
    received = lax.all_to_all(packed, "graph", split_axis=0, concat_axis=0, tiled=True)
    like = lambda array: jax.ShapeDtypeStruct(array.shape, array.dtype)
    stay = lambda arrays: [pltpu.with_memory_space_constraint(one, pltpu.HBM) for one in arrays]
    near, far = pl.BlockSpec(memory_space=pltpu.VMEM), pl.BlockSpec(memory_space=pltpu.HBM)
    source, w_down_t = edge_source[None, :], w_down.T
    target, send_edges, return_edges = (
        edge_target[None, :],
        by_lanes(send_edges),
        by_lanes(return_edges),
    )
    edges, atoms = edge_state.shape[0], atom_state.shape[0]
    early = pl.pallas_call(
        ahead_kernel,
        in_specs=[far] * 12,
        out_specs=[near] * 9,
        out_shape=(
            like(edge_state),
            jax.ShapeDtypeStruct((edges, w_edge.shape[1]), jnp.float32),
            jax.ShapeDtypeStruct((edges, atom_sends.shape[0]), bf16),
            like(w_bilinear),
            like(w_source),
            jax.ShapeDtypeStruct((2 * w_up.shape[0], w_up.shape[1]), bf16),
            jax.ShapeDtypeStruct((2 * send_edges.shape[0], LANES), jnp.int32),
            jax.ShapeDtypeStruct((w_residual.shape[0] - 1,) + w_residual.shape[1:], bf16),
            jax.ShapeDtypeStruct((2 * atoms, atom_state.shape[1]), bf16),
        ),
        scratch_shapes=[
            pltpu.VMEM(array.shape, array.dtype) for array in (w_edge, source, w_bilinear, target)
        ]
        + [pltpu.SemaphoreType.DMA((12,))],
        compiler_params=pltpu.CompilerParams(vmem_limit_bytes=8 * 1024 * 1024),
        name="ahead",
    )(
        *stay(
            (
                edge_state,
                w_edge,
                source,
                w_bilinear,
                target,
                atom_state,
                w_source,
                w_down_t,
                send_edges,
                return_edges,
                w_up,
                w_residual,
            )
        )
    )
    return pl.pallas_call(
        main_kernel,
        in_specs=[near] * 10 + [far] * 2,
        out_shape=(like(edge_state), like(atom_state)),
        scratch_shapes=[
            pltpu.VMEM(w_residual.shape[1:], bf16),
            pltpu.VMEM(w_atom.shape, bf16),
            pltpu.SemaphoreType.DMA((2,)),
        ],
        compiler_params=pltpu.CompilerParams(vmem_limit_bytes=32 * 1024 * 1024),
        name="block",
    )(received, *early, *stay((w_residual, w_atom)))


def bilinear_terms(inputs_x, coeffs, keeps, w_bilinear):
    expanded = matmul(inputs_x, w_bilinear)
    expanded = expanded.reshape(inputs_x.shape[0], coeffs.shape[0], -1)
    mixed = jnp.einsum("tkd,kt->td", expanded, coeffs.astype(jnp.float32))
    return mixed * keeps.astype(jnp.float32)[:, None]


def tile_sums(slot_rows, local_in, local_out, keeps, coeffs, w_bilinear):
    trip_count = slot_rows.shape[0]
    block_size = WIN
    block_count = trip_count // block_size
    basis_rows = coeffs.shape[0]
    block_iota = jnp.arange(block_size, dtype=jnp.int32)

    def one_block(operands):
        rows_blk, in_blk, out_blk, keep_blk, coef_blk = operands
        in_hot = ((in_blk % block_size)[:, None] == block_iota[None, :]).astype(jnp.bfloat16)
        inputs_x = matmul(in_hot, rows_blk).astype(jnp.bfloat16)
        mixed = bilinear_terms(inputs_x, coef_blk, keep_blk, w_bilinear)
        out_hot = (block_iota[:, None] == (out_blk % block_size)[None, :]).astype(jnp.float32)
        return jnp.dot(
            out_hot, mixed, precision=lax.Precision.HIGHEST, preferred_element_type=jnp.float32
        )

    shaped_coeffs = jnp.transpose(coeffs.reshape(basis_rows, block_count, block_size), (1, 0, 2))
    summed = lax.map(
        one_block,
        (
            slot_rows.reshape(block_count, block_size, -1),
            local_in.reshape(block_count, block_size),
            local_out.reshape(block_count, block_size),
            keeps.reshape(block_count, block_size),
            shaped_coeffs,
        ),
    )
    return summed.reshape(trip_count, -1).astype(jnp.bfloat16)


def on_tiles(
    edge_state,
    atom_state,
    atom_sends,
    edge_source,
    edge_target,
    send_edges,
    triplet_in,
    triplet_out,
    triplet_valid,
    triplet_basis,
    return_edges,
    w_edge,
    w_source,
    w_down,
    w_bilinear,
    w_up,
    w_residual,
    w_atom,
):
    edge_count = edge_state.shape[0]
    atom_count = atom_state.shape[0]
    arrived_atoms = lax.all_to_all(
        pick_rows(atom_sends, atom_state), "graph", split_axis=0, concat_axis=0, tiled=True
    )
    src_rows = pick_rows(edge_source, arrived_atoms)
    pre_act = matmul(edge_state, w_edge) + matmul(src_rows, w_source)
    activated = jax.nn.silu(pre_act).astype(jnp.bfloat16)
    projected = jax.nn.silu(matmul(activated, w_down)).astype(jnp.bfloat16)
    slot_rows = lax.all_to_all(
        pick_rows(send_edges, projected), "graph", split_axis=0, concat_axis=0, tiled=True
    )
    slot_sums = tile_sums(
        slot_rows, triplet_in, triplet_out, triplet_valid, triplet_basis, w_bilinear
    )
    returned = lax.all_to_all(slot_sums, "graph", split_axis=0, concat_axis=0, tiled=True)
    back_hot = (jnp.arange(edge_count, dtype=jnp.int32)[:, None] == return_edges[None, :]).astype(
        jnp.bfloat16
    )
    aggregate = matmul(back_hot, returned)
    update = jax.nn.silu(matmul(aggregate.astype(jnp.bfloat16), w_up))
    base = ((edge_state.astype(jnp.float32) + activated.astype(jnp.float32)) * inv_root).astype(
        jnp.bfloat16
    )
    inner_one = jax.nn.silu(matmul(base, w_residual[0])).astype(jnp.bfloat16)
    middle = (
        (base.astype(jnp.float32) + jax.nn.silu(matmul(inner_one, w_residual[1]))) * inv_root
    ).astype(jnp.bfloat16)
    inner_two = jax.nn.silu(matmul(middle, w_residual[2])).astype(jnp.bfloat16)
    chain = (middle.astype(jnp.float32) + jax.nn.silu(matmul(inner_two, w_residual[3]))) * inv_root
    edge_out = (chain + update).astype(jnp.bfloat16)
    contrib = matmul(edge_out, w_atom).astype(jnp.bfloat16)
    one_hot = (edge_target[None, :] == jnp.arange(atom_count, dtype=jnp.int32)[:, None]).astype(
        jnp.bfloat16
    )
    atom_sum = matmul(one_hot, contrib)
    atom_out = (atom_state.astype(jnp.float32) + jax.nn.silu(0.25 * atom_sum)).astype(jnp.bfloat16)
    return (edge_out, atom_out)


def on_device(*arguments):
    peers = lax.axis_size("graph")
    if arguments[5].shape[0] == peers * WIN:
        return local_blocks(peers, *arguments)
    return on_tiles(*arguments)


def solution(mesh):
    placed = (
        P(("groups", "graph"), None),
        P(("groups", "graph"), None),
        P(("groups", "graph")),
        P(("groups", "graph")),
        P(("groups", "graph")),
        P(("groups", "graph")),
        P(("groups", "graph")),
        P(("groups", "graph")),
        P(("groups", "graph")),
        P(None, ("groups", "graph")),
        P(("groups", "graph")),
        P(),
        P(),
        P(),
        P(),
        P(),
        P(),
        P(),
    )
    return jax.shard_map(
        on_device,
        mesh=mesh,
        in_specs=placed,
        out_specs=(P(("groups", "graph"), None), P(("groups", "graph"), None)),
        check_vma=False,
    )
```

```python
import jax
import jax.numpy as jnp
from jax import lax
from jax.experimental import pallas as pl
from jax.experimental.pallas import tpu as pltpu
from jax.sharding import PartitionSpec as P

WIN = 512
LANES = 128
GROWN = 6


inv_root = 0.7071067811865476


def matmul(left, right):
    return jnp.dot(left, right, preferred_element_type=jnp.float32)


def pick_rows(indices, table):
    chooser = (indices[:, None] == jnp.arange(table.shape[0], dtype=jnp.int32)[None, :]).astype(
        table.dtype
    )
    return matmul(chooser, table).astype(table.dtype)


def silu(v):
    return (0.5 * v) * (1.0 + jnp.tanh(0.5 * v))


def pack_kernel(basis_ref, valid_ref, in_ref, out_ref, atom_ref, sends_ref, send_ref):
    basis_rows = basis_ref.shape[0]
    peers = send_ref.shape[0]
    pieces = valid_ref.shape[0] // peers
    width = pieces * LANES
    atom_slots = sends_ref.shape[1]
    cap_a = atom_slots // peers
    chooser = (
        lax.broadcasted_iota(jnp.int32, (atom_ref.shape[0], atom_slots), 0) == sends_ref[...]
    ).astype(jnp.float32).astype(jnp.bfloat16)
    rows = lax.dot_general(
        chooser, atom_ref[...], (((0,), (0,)), ((), ())), preferred_element_type=jnp.float32
    ).astype(jnp.bfloat16)
    keeps = valid_ref[...].astype(jnp.float32)
    half = width // 2
    local_in = ((in_ref[...] % width) - half).astype(jnp.float32).astype(jnp.bfloat16)
    local_out = ((out_ref[...] % width) - half).astype(jnp.float32).astype(jnp.bfloat16)
    for peer in range(peers):
        parts = []
        for piece in range(pieces):
            row = peer * pieces + piece
            tile = basis_ref[:, row * LANES : (row + 1) * LANES].astype(jnp.float32)
            parts.append((tile * keeps[row : row + 1, :]).astype(jnp.bfloat16))
        parts.append(local_in[peer * pieces : (peer + 1) * pieces, :])
        parts.append(local_out[peer * pieces : (peer + 1) * pieces, :])
        for first in range(0, atom_ref.shape[1], LANES):
            parts.append(rows[peer * cap_a : (peer + 1) * cap_a, first : first + LANES])
        send_ref[peer] = jnp.concatenate(parts, axis=0)


def ahead_kernel(
    edge_far,
    w_edge_far,
    source_far,
    w_bilinear_far,
    target_far,
    atom_far,
    w_source_far,
    w_down_t_far,
    send_far,
    return_far,
    w_up_far,
    w_residual_far,
    edge_ref,
    pre_ref,
    source_hot_ref,
    w_mix_ref,
    w_grow_ref,
    w_source_ref,
    w_narrow_ref,
    index_ref,
    w_residual_ref,
    atom_rows_ref,
    w_edge_ref,
    source_ref,
    w_bilinear_ref,
    target_ref,
    sems,
):
    f32, bf16 = jnp.float32, jnp.bfloat16
    slots, narrow, atoms = send_far.shape[0], w_down_t_far.shape[0], atom_far.shape[0]
    copies = [
        pltpu.make_async_copy(here, there, sems.at[at])
        for at, (here, there) in enumerate(
            (
                (edge_far, edge_ref),
                (w_edge_far, w_edge_ref),
                (source_far, source_ref),
                (w_bilinear_far, w_bilinear_ref),
                (target_far, target_ref),
                (atom_far, atom_rows_ref.at[pl.ds(0, atoms), :]),
                (w_source_far, w_source_ref),
                (w_down_t_far, w_narrow_ref.at[pl.ds(0, narrow), :]),
                (w_up_far, w_narrow_ref.at[pl.ds(narrow, narrow), :]),
                (send_far, index_ref.at[pl.ds(0, slots), :]),
                (return_far, index_ref.at[pl.ds(slots, slots), :]),
                (w_residual_far.at[pl.ds(0, w_residual_ref.shape[0])], w_residual_ref),
            )
        )
    ]
    for copy in copies:
        copy.start()
    for copy in copies[:5]:
        copy.wait()
    pre_ref[...] = matmul(edge_ref[...], w_edge_ref[...])
    grown = w_grow_ref.shape[0]
    for first in range(0, w_bilinear_ref.shape[1], 2 * narrow):
        pair = [
            w_bilinear_ref[:, at : at + narrow].astype(f32).T for at in (first, first + narrow)
        ]
        if first < grown:
            w_grow_ref[first : first + 2 * narrow, :] = jnp.concatenate(pair, axis=0).astype(bf16)
        else:
            w_mix_ref[:, first - grown : first - grown + 2 * narrow] = jnp.concatenate(
                pair, axis=1
            ).astype(bf16)
    hot = lax.broadcasted_iota(jnp.int32, source_hot_ref.shape[::-1], 0) == source_ref[...]
    source_hot_ref[...] = hot.astype(f32).T.astype(bf16)
    hot = lax.broadcasted_iota(jnp.int32, (atoms, target_ref.shape[1]), 0) == target_ref[...]
    atom_rows_ref[atoms:, :] = hot.astype(f32).astype(bf16)
    for copy in copies[5:]:
        copy.wait()


def main_kernel(
    recv_ref,
    edge_ref,
    pre_ref,
    source_hot_ref,
    w_mix_ref,
    w_grow_ref,
    w_source_ref,
    w_narrow_ref,
    index_ref,
    w_residual_ref,
    atom_rows_ref,
    w_last_far,
    w_atom_far,
    edge_out_ref,
    atom_out_ref,
    w_last_ref,
    w_atom_ref,
    sems,
):
    copies = [
        pltpu.make_async_copy(w_last_far.at[w_residual_ref.shape[0]], w_last_ref, sems.at[0]),
        pltpu.make_async_copy(w_atom_far, w_atom_ref, sems.at[1]),
    ]
    for copy in copies:
        copy.start()
    bf16, f32 = jnp.bfloat16, jnp.float32
    peers = recv_ref.shape[0]
    slot_rows = index_ref.shape[0] // 2
    pieces = slot_rows // peers
    width = pieces * LANES
    edge_count = edge_ref.shape[0]
    proj_width = w_mix_ref.shape[0]
    atom_count = atom_out_ref.shape[0]
    grown = w_grow_ref.shape[0] // proj_width
    basis_rows = w_mix_ref.shape[1] // proj_width + grown
    index_row = basis_rows * pieces
    atom_row = index_row + 2 * pieces
    halves = atom_out_ref.shape[1] // LANES
    cap_a = (recv_ref.shape[1] - atom_row) // halves

    arrived = jnp.concatenate(
        [
            jnp.concatenate(
                [
                    recv_ref[s, atom_row + h * cap_a : atom_row + (h + 1) * cap_a, :]
                    for s in range(peers)
                ],
                axis=0,
            )
            for h in range(halves)
        ],
        axis=1,
    )
    src_rows = matmul(source_hot_ref[...], arrived).astype(bf16)
    edge = edge_ref[...]
    activated = silu(pre_ref[...] + matmul(src_rows, w_source_ref[...])).astype(bf16)
    projected = silu(
        lax.dot_general(
            w_narrow_ref[:proj_width, :], activated, (((1,), (1,)), ((), ())), preferred_element_type=f32
        )
    ).astype(bf16)
    w_mix = w_mix_ref[...]
    table = jnp.concatenate(
        [projected, matmul(w_grow_ref[...], projected).astype(bf16)], axis=0
    )

    edge_iota = lax.broadcasted_iota(jnp.int32, (edge_count, LANES), 0).astype(f32).astype(bf16)
    packed = 16
    upper = lax.broadcasted_iota(jnp.int32, (2 * pieces, LANES), 0) < pieces
    one, zero = jnp.ones((), bf16), jnp.zeros((), bf16)

    def one_hot(rows):
        parts = []
        for piece in range(pieces):
            spread = jnp.broadcast_to(rows[piece : piece + 1, :], (packed, LANES)).astype(bf16)
            spread = jnp.concatenate([spread] * (edge_count // packed), axis=0)
            parts.append(jnp.where(spread == edge_iota, one, zero))
        return jnp.concatenate(parts, axis=1)

    middle = ((edge.astype(f32) + activated.astype(f32)) * inv_root).astype(bf16)
    inner, stage = None, 0

    def basis_of(t):
        return jnp.concatenate(
            [
                recv_ref[t, piece * basis_rows : (piece + 1) * basis_rows, :]
                for piece in range(pieces)
            ],
            axis=1,
        )

    def choose(t):
        slots = recv_ref[t, index_row:atom_row, :].astype(f32).astype(jnp.int32) + width // 2
        lane, row = slots % LANES, slots // LANES
        found = jnp.zeros(slots.shape, jnp.int32)
        for r in range(pieces):
            here = t * pieces + r
            places = jnp.where(
                upper,
                jnp.broadcast_to(index_ref[here : here + 1, :], slots.shape),
                jnp.broadcast_to(
                    index_ref[slot_rows + here : slot_rows + here + 1, :], slots.shape
                ),
            )
            got = jnp.take_along_axis(places, lane, axis=1, mode="promise_in_bounds")
            found = jnp.where(row == r, got, found)
        found = found.astype(f32)
        rows = matmul(table, one_hot(found[:pieces]))
        near = None
        coeffs = basis_of(t)
        for k in range(grown):
            term = rows[(k + 1) * proj_width : (k + 2) * proj_width, :] * coeffs[
                k : k + 1, :
            ].astype(f32)
            near = term if near is None else near + term
        return rows[:proj_width].astype(bf16), found[pieces:], near

    def mix(t, rows, near):
        coeffs = basis_of(t)
        terms = jnp.concatenate(
            [rows * coeffs[k : k + 1, :] for k in range(grown, basis_rows)], axis=0
        )
        return (matmul(w_mix, terms) + near).astype(bf16)

    def spread(mixed, targets):
        return lax.dot_general(
            one_hot(targets), mixed, (((1,), (1,)), ((), ())), preferred_element_type=f32
        )

    total = jnp.zeros((edge_count, proj_width), f32)
    chosen, mixes = {}, {}
    for step in range(peers + 2):
        if step < peers:
            chosen[step] = choose(step)
        if 0 <= step - 1 < peers:
            mixes[step - 1] = mix(step - 1, chosen[step - 1][0], chosen[step - 1][2])
        if 0 <= step - 2 < peers:
            total = total + spread(mixes.pop(step - 2), chosen.pop(step - 2)[1])
        if step < peers and (step + 1) * w_residual_ref.shape[0] // peers > stage:
            fresh = silu(matmul(middle if stage % 2 == 0 else inner, w_residual_ref[stage]))
            if stage % 2 == 0:
                inner = fresh.astype(bf16)
            else:
                middle = ((middle.astype(f32) + fresh) * inv_root).astype(bf16)
            stage += 1
    for copy in copies:
        copy.wait()
    chain = (middle.astype(f32) + silu(matmul(inner, w_last_ref[...]))) * inv_root
    update = silu(matmul(total.astype(bf16), w_narrow_ref[proj_width:, :]))
    edge_out = (chain + update).astype(bf16)
    edge_out_ref[...] = edge_out
    contrib = matmul(edge_out, w_atom_ref[...]).astype(bf16)
    atom_sum = matmul(atom_rows_ref[atom_count:, :], contrib)
    atom_out_ref[...] = (
        atom_rows_ref[:atom_count, :].astype(f32) + silu(0.25 * atom_sum)
    ).astype(bf16)


def local_blocks(
    peers,
    edge_state,
    atom_state,
    atom_sends,
    edge_source,
    edge_target,
    send_edges,
    triplet_in,
    triplet_out,
    triplet_valid,
    triplet_basis,
    return_edges,
    w_edge,
    w_source,
    w_down,
    w_bilinear,
    w_up,
    w_residual,
    w_atom,
):
    bf16 = jnp.bfloat16
    pieces = WIN // LANES
    rows = triplet_basis.shape[0] * pieces + 2 * pieces
    rows += atom_sends.shape[0] // peers * (atom_state.shape[1] // LANES)
    by_lanes = lambda array: array.reshape(-1, LANES)
    packed = pl.pallas_call(
        pack_kernel,
        out_shape=jax.ShapeDtypeStruct((peers, rows, LANES), bf16),
        name="pack",
    )(
        triplet_basis,
        by_lanes(triplet_valid),
        by_lanes(triplet_in),
        by_lanes(triplet_out),
        atom_state,
        atom_sends[None, :],
    )
    received = lax.all_to_all(packed, "graph", split_axis=0, concat_axis=0, tiled=True)
    like = lambda array: jax.ShapeDtypeStruct(array.shape, array.dtype)
    stay = lambda arrays: [pltpu.with_memory_space_constraint(one, pltpu.HBM) for one in arrays]
    near, far = pl.BlockSpec(memory_space=pltpu.VMEM), pl.BlockSpec(memory_space=pltpu.HBM)
    source, w_down_t = edge_source[None, :], w_down.T
    target, send_edges, return_edges = (
        edge_target[None, :],
        by_lanes(send_edges),
        by_lanes(return_edges),
    )
    edges, atoms = edge_state.shape[0], atom_state.shape[0]
    narrow = w_up.shape[0]
    grown = GROWN * narrow
    early = pl.pallas_call(
        ahead_kernel,
        in_specs=[far] * 12,
        out_specs=[near] * 10,
        out_shape=(
            like(edge_state),
            jax.ShapeDtypeStruct((edges, w_edge.shape[1]), jnp.float32),
            jax.ShapeDtypeStruct((edges, atom_sends.shape[0]), bf16),
            jax.ShapeDtypeStruct((narrow, w_bilinear.shape[1] - grown), bf16),
            jax.ShapeDtypeStruct((grown, narrow), bf16),
            like(w_source),
            jax.ShapeDtypeStruct((2 * w_up.shape[0], w_up.shape[1]), bf16),
            jax.ShapeDtypeStruct((2 * send_edges.shape[0], LANES), jnp.int32),
            jax.ShapeDtypeStruct((w_residual.shape[0] - 1,) + w_residual.shape[1:], bf16),
            jax.ShapeDtypeStruct((2 * atoms, atom_state.shape[1]), bf16),
        ),
        scratch_shapes=[
            pltpu.VMEM(array.shape, array.dtype) for array in (w_edge, source, w_bilinear, target)
        ]
        + [pltpu.SemaphoreType.DMA((12,))],
        compiler_params=pltpu.CompilerParams(vmem_limit_bytes=8 * 1024 * 1024),
        name="ahead",
    )(
        *stay(
            (
                edge_state,
                w_edge,
                source,
                w_bilinear,
                target,
                atom_state,
                w_source,
                w_down_t,
                send_edges,
                return_edges,
                w_up,
                w_residual,
            )
        )
    )
    return pl.pallas_call(
        main_kernel,
        in_specs=[near] * 11 + [far] * 2,
        out_shape=(like(edge_state), like(atom_state)),
        scratch_shapes=[
            pltpu.VMEM(w_residual.shape[1:], bf16),
            pltpu.VMEM(w_atom.shape, bf16),
            pltpu.SemaphoreType.DMA((2,)),
        ],
        compiler_params=pltpu.CompilerParams(vmem_limit_bytes=32 * 1024 * 1024),
        name="block",
    )(received, *early, *stay((w_residual, w_atom)))


def bilinear_terms(inputs_x, coeffs, keeps, w_bilinear):
    expanded = matmul(inputs_x, w_bilinear)
    expanded = expanded.reshape(inputs_x.shape[0], coeffs.shape[0], -1)
    mixed = jnp.einsum("tkd,kt->td", expanded, coeffs.astype(jnp.float32))
    return mixed * keeps.astype(jnp.float32)[:, None]


def tile_sums(slot_rows, local_in, local_out, keeps, coeffs, w_bilinear):
    trip_count = slot_rows.shape[0]
    block_size = WIN
    block_count = trip_count // block_size
    basis_rows = coeffs.shape[0]
    block_iota = jnp.arange(block_size, dtype=jnp.int32)

    def one_block(operands):
        rows_blk, in_blk, out_blk, keep_blk, coef_blk = operands
        in_hot = ((in_blk % block_size)[:, None] == block_iota[None, :]).astype(jnp.bfloat16)
        inputs_x = matmul(in_hot, rows_blk).astype(jnp.bfloat16)
        mixed = bilinear_terms(inputs_x, coef_blk, keep_blk, w_bilinear)
        out_hot = (block_iota[:, None] == (out_blk % block_size)[None, :]).astype(jnp.float32)
        return jnp.dot(
            out_hot, mixed, precision=lax.Precision.HIGHEST, preferred_element_type=jnp.float32
        )

    shaped_coeffs = jnp.transpose(coeffs.reshape(basis_rows, block_count, block_size), (1, 0, 2))
    summed = lax.map(
        one_block,
        (
            slot_rows.reshape(block_count, block_size, -1),
            local_in.reshape(block_count, block_size),
            local_out.reshape(block_count, block_size),
            keeps.reshape(block_count, block_size),
            shaped_coeffs,
        ),
    )
    return summed.reshape(trip_count, -1).astype(jnp.bfloat16)


def on_tiles(
    edge_state,
    atom_state,
    atom_sends,
    edge_source,
    edge_target,
    send_edges,
    triplet_in,
    triplet_out,
    triplet_valid,
    triplet_basis,
    return_edges,
    w_edge,
    w_source,
    w_down,
    w_bilinear,
    w_up,
    w_residual,
    w_atom,
):
    edge_count = edge_state.shape[0]
    atom_count = atom_state.shape[0]
    arrived_atoms = lax.all_to_all(
        pick_rows(atom_sends, atom_state), "graph", split_axis=0, concat_axis=0, tiled=True
    )
    src_rows = pick_rows(edge_source, arrived_atoms)
    pre_act = matmul(edge_state, w_edge) + matmul(src_rows, w_source)
    activated = jax.nn.silu(pre_act).astype(jnp.bfloat16)
    projected = jax.nn.silu(matmul(activated, w_down)).astype(jnp.bfloat16)
    slot_rows = lax.all_to_all(
        pick_rows(send_edges, projected), "graph", split_axis=0, concat_axis=0, tiled=True
    )
    slot_sums = tile_sums(
        slot_rows, triplet_in, triplet_out, triplet_valid, triplet_basis, w_bilinear
    )
    returned = lax.all_to_all(slot_sums, "graph", split_axis=0, concat_axis=0, tiled=True)
    back_hot = (jnp.arange(edge_count, dtype=jnp.int32)[:, None] == return_edges[None, :]).astype(
        jnp.bfloat16
    )
    aggregate = matmul(back_hot, returned)
    update = jax.nn.silu(matmul(aggregate.astype(jnp.bfloat16), w_up))
    base = ((edge_state.astype(jnp.float32) + activated.astype(jnp.float32)) * inv_root).astype(
        jnp.bfloat16
    )
    inner_one = jax.nn.silu(matmul(base, w_residual[0])).astype(jnp.bfloat16)
    middle = (
        (base.astype(jnp.float32) + jax.nn.silu(matmul(inner_one, w_residual[1]))) * inv_root
    ).astype(jnp.bfloat16)
    inner_two = jax.nn.silu(matmul(middle, w_residual[2])).astype(jnp.bfloat16)
    chain = (middle.astype(jnp.float32) + jax.nn.silu(matmul(inner_two, w_residual[3]))) * inv_root
    edge_out = (chain + update).astype(jnp.bfloat16)
    contrib = matmul(edge_out, w_atom).astype(jnp.bfloat16)
    one_hot = (edge_target[None, :] == jnp.arange(atom_count, dtype=jnp.int32)[:, None]).astype(
        jnp.bfloat16
    )
    atom_sum = matmul(one_hot, contrib)
    atom_out = (atom_state.astype(jnp.float32) + jax.nn.silu(0.25 * atom_sum)).astype(jnp.bfloat16)
    return (edge_out, atom_out)


def on_device(*arguments):
    peers = lax.axis_size("graph")
    if arguments[5].shape[0] == peers * WIN:
        return local_blocks(peers, *arguments)
    return on_tiles(*arguments)


def solution(mesh):
    placed = (
        P(("groups", "graph"), None),
        P(("groups", "graph"), None),
        P(("groups", "graph")),
        P(("groups", "graph")),
        P(("groups", "graph")),
        P(("groups", "graph")),
        P(("groups", "graph")),
        P(("groups", "graph")),
        P(("groups", "graph")),
        P(None, ("groups", "graph")),
        P(("groups", "graph")),
        P(),
        P(),
        P(),
        P(),
        P(),
        P(),
        P(),
    )
    return jax.shard_map(
        on_device,
        mesh=mesh,
        in_specs=placed,
        out_specs=(P(("groups", "graph"), None), P(("groups", "graph"), None)),
        check_vma=False,
    )
```

```python
import jax
import jax.numpy as jnp
from jax import lax
from jax.experimental import pallas as pl
from jax.experimental.pallas import tpu as pltpu
from jax.sharding import PartitionSpec as P

WIN = 512
LANES = 128
GROWN = 6


inv_root = 0.7071067811865476


def matmul(left, right):
    return jnp.dot(left, right, preferred_element_type=jnp.float32)


def pick_rows(indices, table):
    chooser = (indices[:, None] == jnp.arange(table.shape[0], dtype=jnp.int32)[None, :]).astype(
        table.dtype
    )
    return matmul(chooser, table).astype(table.dtype)


def silu(v):
    return (0.5 * v) * (1.0 + jnp.tanh(0.5 * v))


def pack_kernel(
    basis_far,
    valid_far,
    in_far,
    out_far,
    atom_far,
    sends_far,
    send_far,
    basis_ref,
    valid_ref,
    in_ref,
    out_ref,
    atom_ref,
    sends_ref,
    send_ref,
    sems,
    done_sems,
):
    peers, parts = send_ref.shape[0], done_sems.shape[0]
    span, columns = peers // parts, basis_ref.shape[1] // parts
    copies = [
        pltpu.make_async_copy(here, there, sems.at[at])
        for at, (here, there) in enumerate(
            [
                (atom_far, atom_ref),
                (sends_far, sends_ref),
                (valid_far, valid_ref),
                (in_far, in_ref),
                (out_far, out_ref),
            ]
            + [
                (
                    basis_far.at[:, pl.ds(part * columns, columns)],
                    basis_ref.at[:, pl.ds(part * columns, columns)],
                )
                for part in range(parts)
            ]
        )
    ]
    for copy in copies:
        copy.start()
    for copy in copies[:5]:
        copy.wait()
    pieces = valid_ref.shape[0] // peers
    width = pieces * LANES
    atom_slots = sends_ref.shape[1]
    cap_a = atom_slots // peers
    chooser = (
        lax.broadcasted_iota(jnp.int32, (atom_ref.shape[0], atom_slots), 0) == sends_ref[...]
    ).astype(jnp.float32).astype(jnp.bfloat16)
    rows = lax.dot_general(
        chooser, atom_ref[...], (((0,), (0,)), ((), ())), preferred_element_type=jnp.float32
    ).astype(jnp.bfloat16)
    keeps = valid_ref[...].astype(jnp.float32).astype(jnp.bfloat16)
    half = width // 2
    local_in = ((in_ref[...] % width) - half).astype(jnp.float32).astype(jnp.bfloat16)
    local_out = ((out_ref[...] % width) - half).astype(jnp.float32).astype(jnp.bfloat16)
    sent = []
    for part in range(parts):
        copies[5 + part].wait()
        for peer in range(part * span, (part + 1) * span):
            blocks = []
            for piece in range(pieces):
                row = peer * pieces + piece
                blocks.append(basis_ref[:, row * LANES : (row + 1) * LANES] * keeps[row : row + 1, :])
            blocks.append(local_in[peer * pieces : (peer + 1) * pieces, :])
            blocks.append(local_out[peer * pieces : (peer + 1) * pieces, :])
            for first in range(0, atom_ref.shape[1], LANES):
                blocks.append(rows[peer * cap_a : (peer + 1) * cap_a, first : first + LANES])
            send_ref[peer] = jnp.concatenate(blocks, axis=0)
        sent.append(
            pltpu.make_async_copy(
                send_ref.at[pl.ds(part * span, span)],
                send_far.at[pl.ds(part * span, span)],
                done_sems.at[part],
            )
        )
        sent[-1].start()
    for copy in sent:
        copy.wait()


def ahead_kernel(
    edge_far,
    w_edge_far,
    source_far,
    w_bilinear_far,
    target_far,
    atom_far,
    w_source_far,
    w_down_t_far,
    send_far,
    return_far,
    w_up_far,
    w_residual_far,
    edge_ref,
    pre_ref,
    source_hot_ref,
    w_mix_ref,
    w_grow_ref,
    w_source_ref,
    w_narrow_ref,
    index_ref,
    w_residual_ref,
    atom_rows_ref,
    w_edge_ref,
    source_ref,
    w_bilinear_ref,
    target_ref,
    sems,
):
    f32, bf16 = jnp.float32, jnp.bfloat16
    slots, narrow, atoms = send_far.shape[0], w_down_t_far.shape[0], atom_far.shape[0]
    copies = [
        pltpu.make_async_copy(here, there, sems.at[at])
        for at, (here, there) in enumerate(
            (
                (edge_far, edge_ref),
                (w_edge_far, w_edge_ref),
                (source_far, source_ref),
                (w_bilinear_far, w_bilinear_ref),
                (target_far, target_ref),
                (atom_far, atom_rows_ref.at[pl.ds(0, atoms), :]),
                (w_source_far, w_source_ref),
                (w_down_t_far, w_narrow_ref.at[pl.ds(0, narrow), :]),
                (w_up_far, w_narrow_ref.at[pl.ds(narrow, narrow), :]),
                (send_far, index_ref.at[pl.ds(0, slots), :]),
                (return_far, index_ref.at[pl.ds(slots, slots), :]),
                (w_residual_far.at[pl.ds(0, w_residual_ref.shape[0])], w_residual_ref),
            )
        )
    ]
    for copy in copies:
        copy.start()
    for copy in copies[:5]:
        copy.wait()
    pre_ref[...] = matmul(edge_ref[...], w_edge_ref[...])
    grown = w_grow_ref.shape[0]
    for first in range(0, w_bilinear_ref.shape[1], 2 * narrow):
        pair = [
            w_bilinear_ref[:, at : at + narrow].astype(f32).T for at in (first, first + narrow)
        ]
        if first < grown:
            w_grow_ref[first : first + 2 * narrow, :] = jnp.concatenate(pair, axis=0).astype(bf16)
        else:
            w_mix_ref[:, first - grown : first - grown + 2 * narrow] = jnp.concatenate(
                pair, axis=1
            ).astype(bf16)
    hot = lax.broadcasted_iota(jnp.int32, source_hot_ref.shape[::-1], 0) == source_ref[...]
    source_hot_ref[...] = hot.astype(f32).T.astype(bf16)
    hot = lax.broadcasted_iota(jnp.int32, (atoms, target_ref.shape[1]), 0) == target_ref[...]
    atom_rows_ref[atoms:, :] = hot.astype(f32).astype(bf16)
    for copy in copies[5:]:
        copy.wait()


def main_kernel(
    recv_ref,
    edge_ref,
    pre_ref,
    source_hot_ref,
    w_mix_ref,
    w_grow_ref,
    w_source_ref,
    w_narrow_ref,
    index_ref,
    w_residual_ref,
    atom_rows_ref,
    w_last_far,
    w_atom_far,
    edge_out_ref,
    atom_out_ref,
    w_last_ref,
    w_atom_ref,
    sems,
):
    copies = [
        pltpu.make_async_copy(w_last_far.at[w_residual_ref.shape[0]], w_last_ref, sems.at[0]),
        pltpu.make_async_copy(w_atom_far, w_atom_ref, sems.at[1]),
    ]
    for copy in copies:
        copy.start()
    bf16, f32 = jnp.bfloat16, jnp.float32
    peers = recv_ref.shape[0]
    slot_rows = index_ref.shape[0] // 2
    pieces = slot_rows // peers
    width = pieces * LANES
    edge_count = edge_ref.shape[0]
    proj_width = w_mix_ref.shape[0]
    atom_count = atom_out_ref.shape[0]
    grown = w_grow_ref.shape[0] // proj_width
    basis_rows = w_mix_ref.shape[1] // proj_width + grown
    index_row = basis_rows * pieces
    atom_row = index_row + 2 * pieces
    halves = atom_out_ref.shape[1] // LANES
    cap_a = (recv_ref.shape[1] - atom_row) // halves

    arrived = jnp.concatenate(
        [
            jnp.concatenate(
                [
                    recv_ref[s, atom_row + h * cap_a : atom_row + (h + 1) * cap_a, :]
                    for s in range(peers)
                ],
                axis=0,
            )
            for h in range(halves)
        ],
        axis=1,
    )
    src_rows = matmul(source_hot_ref[...], arrived).astype(bf16)
    edge = edge_ref[...]
    activated = silu(pre_ref[...] + matmul(src_rows, w_source_ref[...])).astype(bf16)
    projected = silu(
        lax.dot_general(
            w_narrow_ref[:proj_width, :], activated, (((1,), (1,)), ((), ())), preferred_element_type=f32
        )
    ).astype(bf16)
    w_mix = w_mix_ref[...]
    table = jnp.concatenate(
        [projected, matmul(w_grow_ref[...], projected).astype(bf16)], axis=0
    )

    edge_iota = lax.broadcasted_iota(jnp.int32, (edge_count, LANES), 0).astype(f32).astype(bf16)
    packed = 16
    upper = lax.broadcasted_iota(jnp.int32, (2 * pieces, LANES), 0) < pieces
    one, zero = jnp.ones((), bf16), jnp.zeros((), bf16)

    def one_hot(rows):
        parts = []
        for piece in range(pieces):
            spread = jnp.broadcast_to(rows[piece : piece + 1, :], (packed, LANES)).astype(bf16)
            spread = jnp.concatenate([spread] * (edge_count // packed), axis=0)
            parts.append(jnp.where(spread == edge_iota, one, zero))
        return jnp.concatenate(parts, axis=1)

    middle = ((edge.astype(f32) + activated.astype(f32)) * inv_root).astype(bf16)
    inner, stage = None, 0

    def basis_of(t):
        return jnp.concatenate(
            [
                recv_ref[t, piece * basis_rows : (piece + 1) * basis_rows, :]
                for piece in range(pieces)
            ],
            axis=1,
        )

    def choose(t):
        slots = recv_ref[t, index_row:atom_row, :].astype(f32).astype(jnp.int32) + width // 2
        lane, row = slots % LANES, slots // LANES
        found = jnp.zeros(slots.shape, jnp.int32)
        for r in range(pieces):
            here = t * pieces + r
            places = jnp.where(
                upper,
                jnp.broadcast_to(index_ref[here : here + 1, :], slots.shape),
                jnp.broadcast_to(
                    index_ref[slot_rows + here : slot_rows + here + 1, :], slots.shape
                ),
            )
            got = jnp.take_along_axis(places, lane, axis=1, mode="promise_in_bounds")
            found = jnp.where(row == r, got, found)
        found = found.astype(f32)
        rows = matmul(table, one_hot(found[:pieces]))
        near = None
        coeffs = basis_of(t)
        for k in range(grown):
            term = rows[(k + 1) * proj_width : (k + 2) * proj_width, :] * coeffs[
                k : k + 1, :
            ].astype(f32)
            near = term if near is None else near + term
        return rows[:proj_width].astype(bf16), one_hot(found[pieces:]), near

    def mix(t, rows, near):
        coeffs = basis_of(t)
        terms = jnp.concatenate(
            [rows * coeffs[k : k + 1, :] for k in range(grown, basis_rows)], axis=0
        )
        return (matmul(w_mix, terms) + near).astype(bf16)

    def spread(mixed, targets):
        return lax.dot_general(
            targets, mixed, (((1,), (1,)), ((), ())), preferred_element_type=f32
        )

    total = jnp.zeros((edge_count, proj_width), f32)
    chosen, mixes = {}, {}
    for step in range(peers + 2):
        if step < peers:
            chosen[step] = choose(step)
        if 0 <= step - 1 < peers:
            mixes[step - 1] = mix(step - 1, chosen[step - 1][0], chosen[step - 1][2])
        if 0 <= step - 2 < peers:
            total = total + spread(mixes.pop(step - 2), chosen.pop(step - 2)[1])
        if step < peers and (step + 1) * w_residual_ref.shape[0] // peers > stage:
            fresh = silu(matmul(middle if stage % 2 == 0 else inner, w_residual_ref[stage]))
            if stage % 2 == 0:
                inner = fresh.astype(bf16)
            else:
                middle = ((middle.astype(f32) + fresh) * inv_root).astype(bf16)
            stage += 1
    for copy in copies:
        copy.wait()
    chain = (middle.astype(f32) + silu(matmul(inner, w_last_ref[...]))) * inv_root
    update = silu(matmul(total.astype(bf16), w_narrow_ref[proj_width:, :]))
    edge_out = (chain + update).astype(bf16)
    edge_out_ref[...] = edge_out
    contrib = matmul(edge_out, w_atom_ref[...]).astype(bf16)
    atom_sum = matmul(atom_rows_ref[atom_count:, :], contrib)
    atom_out_ref[...] = (
        atom_rows_ref[:atom_count, :].astype(f32) + silu(0.25 * atom_sum)
    ).astype(bf16)


def local_blocks(
    peers,
    edge_state,
    atom_state,
    atom_sends,
    edge_source,
    edge_target,
    send_edges,
    triplet_in,
    triplet_out,
    triplet_valid,
    triplet_basis,
    return_edges,
    w_edge,
    w_source,
    w_down,
    w_bilinear,
    w_up,
    w_residual,
    w_atom,
):
    bf16 = jnp.bfloat16
    pieces = WIN // LANES
    rows = triplet_basis.shape[0] * pieces + 2 * pieces
    rows += atom_sends.shape[0] // peers * (atom_state.shape[1] // LANES)
    by_lanes = lambda array: array.reshape(-1, LANES)
    like = lambda array: jax.ShapeDtypeStruct(array.shape, array.dtype)
    stay = lambda arrays: [pltpu.with_memory_space_constraint(one, pltpu.HBM) for one in arrays]
    near, far = pl.BlockSpec(memory_space=pltpu.VMEM), pl.BlockSpec(memory_space=pltpu.HBM)
    inputs = (
        triplet_basis,
        by_lanes(triplet_valid),
        by_lanes(triplet_in),
        by_lanes(triplet_out),
        atom_state,
        atom_sends[None, :],
    )
    parts = 4 if peers % 4 == 0 else 1
    packed = pl.pallas_call(
        pack_kernel,
        in_specs=[far] * len(inputs),
        out_specs=far,
        out_shape=jax.ShapeDtypeStruct((peers, rows, LANES), bf16),
        scratch_shapes=[pltpu.VMEM(one.shape, one.dtype) for one in inputs]
        + [
            pltpu.VMEM((peers, rows, LANES), bf16),
            pltpu.SemaphoreType.DMA((len(inputs) - 1 + parts,)),
            pltpu.SemaphoreType.DMA((parts,)),
        ],
        name="pack",
    )(*stay(inputs))
    received = lax.all_to_all(packed, "graph", split_axis=0, concat_axis=0, tiled=True)
    source, w_down_t = edge_source[None, :], w_down.T
    target, send_edges, return_edges = (
        edge_target[None, :],
        by_lanes(send_edges),
        by_lanes(return_edges),
    )
    edges, atoms = edge_state.shape[0], atom_state.shape[0]
    narrow = w_up.shape[0]
    grown = GROWN * narrow
    early = pl.pallas_call(
        ahead_kernel,
        in_specs=[far] * 12,
        out_specs=[near] * 10,
        out_shape=(
            like(edge_state),
            jax.ShapeDtypeStruct((edges, w_edge.shape[1]), jnp.float32),
            jax.ShapeDtypeStruct((edges, atom_sends.shape[0]), bf16),
            jax.ShapeDtypeStruct((narrow, w_bilinear.shape[1] - grown), bf16),
            jax.ShapeDtypeStruct((grown, narrow), bf16),
            like(w_source),
            jax.ShapeDtypeStruct((2 * w_up.shape[0], w_up.shape[1]), bf16),
            jax.ShapeDtypeStruct((2 * send_edges.shape[0], LANES), jnp.int32),
            jax.ShapeDtypeStruct((w_residual.shape[0] - 1,) + w_residual.shape[1:], bf16),
            jax.ShapeDtypeStruct((2 * atoms, atom_state.shape[1]), bf16),
        ),
        scratch_shapes=[
            pltpu.VMEM(array.shape, array.dtype) for array in (w_edge, source, w_bilinear, target)
        ]
        + [pltpu.SemaphoreType.DMA((12,))],
        compiler_params=pltpu.CompilerParams(vmem_limit_bytes=8 * 1024 * 1024),
        name="ahead",
    )(
        *stay(
            (
                edge_state,
                w_edge,
                source,
                w_bilinear,
                target,
                atom_state,
                w_source,
                w_down_t,
                send_edges,
                return_edges,
                w_up,
                w_residual,
            )
        )
    )
    return pl.pallas_call(
        main_kernel,
        in_specs=[near] * 11 + [far] * 2,
        out_shape=(like(edge_state), like(atom_state)),
        scratch_shapes=[
            pltpu.VMEM(w_residual.shape[1:], bf16),
            pltpu.VMEM(w_atom.shape, bf16),
            pltpu.SemaphoreType.DMA((2,)),
        ],
        compiler_params=pltpu.CompilerParams(vmem_limit_bytes=32 * 1024 * 1024),
        name="block",
    )(received, *early, *stay((w_residual, w_atom)))


def bilinear_terms(inputs_x, coeffs, keeps, w_bilinear):
    expanded = matmul(inputs_x, w_bilinear)
    expanded = expanded.reshape(inputs_x.shape[0], coeffs.shape[0], -1)
    mixed = jnp.einsum("tkd,kt->td", expanded, coeffs.astype(jnp.float32))
    return mixed * keeps.astype(jnp.float32)[:, None]


def tile_sums(slot_rows, local_in, local_out, keeps, coeffs, w_bilinear):
    trip_count = slot_rows.shape[0]
    block_size = WIN
    block_count = trip_count // block_size
    basis_rows = coeffs.shape[0]
    block_iota = jnp.arange(block_size, dtype=jnp.int32)

    def one_block(operands):
        rows_blk, in_blk, out_blk, keep_blk, coef_blk = operands
        in_hot = ((in_blk % block_size)[:, None] == block_iota[None, :]).astype(jnp.bfloat16)
        inputs_x = matmul(in_hot, rows_blk).astype(jnp.bfloat16)
        mixed = bilinear_terms(inputs_x, coef_blk, keep_blk, w_bilinear)
        out_hot = (block_iota[:, None] == (out_blk % block_size)[None, :]).astype(jnp.float32)
        return jnp.dot(
            out_hot, mixed, precision=lax.Precision.HIGHEST, preferred_element_type=jnp.float32
        )

    shaped_coeffs = jnp.transpose(coeffs.reshape(basis_rows, block_count, block_size), (1, 0, 2))
    summed = lax.map(
        one_block,
        (
            slot_rows.reshape(block_count, block_size, -1),
            local_in.reshape(block_count, block_size),
            local_out.reshape(block_count, block_size),
            keeps.reshape(block_count, block_size),
            shaped_coeffs,
        ),
    )
    return summed.reshape(trip_count, -1).astype(jnp.bfloat16)


def on_tiles(
    edge_state,
    atom_state,
    atom_sends,
    edge_source,
    edge_target,
    send_edges,
    triplet_in,
    triplet_out,
    triplet_valid,
    triplet_basis,
    return_edges,
    w_edge,
    w_source,
    w_down,
    w_bilinear,
    w_up,
    w_residual,
    w_atom,
):
    edge_count = edge_state.shape[0]
    atom_count = atom_state.shape[0]
    arrived_atoms = lax.all_to_all(
        pick_rows(atom_sends, atom_state), "graph", split_axis=0, concat_axis=0, tiled=True
    )
    src_rows = pick_rows(edge_source, arrived_atoms)
    pre_act = matmul(edge_state, w_edge) + matmul(src_rows, w_source)
    activated = jax.nn.silu(pre_act).astype(jnp.bfloat16)
    projected = jax.nn.silu(matmul(activated, w_down)).astype(jnp.bfloat16)
    slot_rows = lax.all_to_all(
        pick_rows(send_edges, projected), "graph", split_axis=0, concat_axis=0, tiled=True
    )
    slot_sums = tile_sums(
        slot_rows, triplet_in, triplet_out, triplet_valid, triplet_basis, w_bilinear
    )
    returned = lax.all_to_all(slot_sums, "graph", split_axis=0, concat_axis=0, tiled=True)
    back_hot = (jnp.arange(edge_count, dtype=jnp.int32)[:, None] == return_edges[None, :]).astype(
        jnp.bfloat16
    )
    aggregate = matmul(back_hot, returned)
    update = jax.nn.silu(matmul(aggregate.astype(jnp.bfloat16), w_up))
    base = ((edge_state.astype(jnp.float32) + activated.astype(jnp.float32)) * inv_root).astype(
        jnp.bfloat16
    )
    inner_one = jax.nn.silu(matmul(base, w_residual[0])).astype(jnp.bfloat16)
    middle = (
        (base.astype(jnp.float32) + jax.nn.silu(matmul(inner_one, w_residual[1]))) * inv_root
    ).astype(jnp.bfloat16)
    inner_two = jax.nn.silu(matmul(middle, w_residual[2])).astype(jnp.bfloat16)
    chain = (middle.astype(jnp.float32) + jax.nn.silu(matmul(inner_two, w_residual[3]))) * inv_root
    edge_out = (chain + update).astype(jnp.bfloat16)
    contrib = matmul(edge_out, w_atom).astype(jnp.bfloat16)
    one_hot = (edge_target[None, :] == jnp.arange(atom_count, dtype=jnp.int32)[:, None]).astype(
        jnp.bfloat16
    )
    atom_sum = matmul(one_hot, contrib)
    atom_out = (atom_state.astype(jnp.float32) + jax.nn.silu(0.25 * atom_sum)).astype(jnp.bfloat16)
    return (edge_out, atom_out)


def on_device(*arguments):
    peers = lax.axis_size("graph")
    if arguments[5].shape[0] == peers * WIN:
        return local_blocks(peers, *arguments)
    return on_tiles(*arguments)


def solution(mesh):
    placed = (
        P(("groups", "graph"), None),
        P(("groups", "graph"), None),
        P(("groups", "graph")),
        P(("groups", "graph")),
        P(("groups", "graph")),
        P(("groups", "graph")),
        P(("groups", "graph")),
        P(("groups", "graph")),
        P(("groups", "graph")),
        P(None, ("groups", "graph")),
        P(("groups", "graph")),
        P(),
        P(),
        P(),
        P(),
        P(),
        P(),
        P(),
    )
    return jax.shard_map(
        on_device,
        mesh=mesh,
        in_specs=placed,
        out_specs=(P(("groups", "graph"), None), P(("groups", "graph"), None)),
        check_vma=False,
    )
```

```python
import jax
import jax.numpy as jnp
from jax import lax
from jax.experimental import pallas as pl
from jax.experimental.pallas import tpu as pltpu
from jax.sharding import PartitionSpec as P

WIN = 512
LANES = 128
GROWN = 6


inv_root = 0.7071067811865476


def matmul(left, right):
    return jnp.dot(left, right, preferred_element_type=jnp.float32)


def pick_rows(indices, table):
    chooser = (indices[:, None] == jnp.arange(table.shape[0], dtype=jnp.int32)[None, :]).astype(
        table.dtype
    )
    return matmul(chooser, table).astype(table.dtype)


def silu(v):
    return (0.5 * v) * (1.0 + jnp.tanh(0.5 * v))


def pack_kernel(basis_ref, valid_ref, in_ref, out_ref, atom_ref, sends_ref, send_ref):
    basis_rows = basis_ref.shape[0]
    peers = send_ref.shape[0]
    pieces = valid_ref.shape[0] // peers
    width = pieces * LANES
    atom_slots = sends_ref.shape[1]
    cap_a = atom_slots // peers
    chooser = (
        lax.broadcasted_iota(jnp.int32, (atom_ref.shape[0], atom_slots), 0) == sends_ref[...]
    ).astype(jnp.float32).astype(jnp.bfloat16)
    rows = lax.dot_general(
        chooser, atom_ref[...], (((0,), (0,)), ((), ())), preferred_element_type=jnp.float32
    ).astype(jnp.bfloat16)
    keeps = valid_ref[...].astype(jnp.float32)
    half = width // 2
    local_in = ((in_ref[...] % width) - half).astype(jnp.float32).astype(jnp.bfloat16)
    local_out = ((out_ref[...] % width) - half).astype(jnp.float32).astype(jnp.bfloat16)
    for peer in range(peers):
        parts = []
        for piece in range(pieces):
            row = peer * pieces + piece
            tile = basis_ref[:, row * LANES : (row + 1) * LANES].astype(jnp.float32)
            parts.append((tile * keeps[row : row + 1, :]).astype(jnp.bfloat16))
        parts.append(local_in[peer * pieces : (peer + 1) * pieces, :])
        parts.append(local_out[peer * pieces : (peer + 1) * pieces, :])
        for first in range(0, atom_ref.shape[1], LANES):
            parts.append(rows[peer * cap_a : (peer + 1) * cap_a, first : first + LANES])
        send_ref[peer] = jnp.concatenate(parts, axis=0)


def ahead_kernel(
    edge_far,
    w_edge_far,
    source_far,
    w_bilinear_far,
    target_far,
    atom_far,
    w_source_far,
    w_down_t_far,
    send_far,
    return_far,
    w_up_far,
    w_residual_far,
    edge_ref,
    pre_ref,
    source_hot_ref,
    w_mix_ref,
    w_grow_ref,
    w_source_ref,
    w_narrow_ref,
    index_ref,
    w_residual_ref,
    atom_rows_ref,
    w_edge_ref,
    source_ref,
    w_bilinear_ref,
    target_ref,
    sems,
):
    f32, bf16 = jnp.float32, jnp.bfloat16
    slots, narrow, atoms = send_far.shape[0], w_down_t_far.shape[0], atom_far.shape[0]
    copies = [
        pltpu.make_async_copy(here, there, sems.at[at])
        for at, (here, there) in enumerate(
            (
                (edge_far, edge_ref),
                (w_edge_far, w_edge_ref),
                (source_far, source_ref),
                (w_bilinear_far, w_bilinear_ref),
                (target_far, target_ref),
                (atom_far, atom_rows_ref.at[pl.ds(0, atoms), :]),
                (w_source_far, w_source_ref),
                (w_down_t_far, w_narrow_ref.at[pl.ds(0, narrow), :]),
                (w_up_far, w_narrow_ref.at[pl.ds(narrow, narrow), :]),
                (send_far, index_ref.at[pl.ds(0, slots), :]),
                (return_far, index_ref.at[pl.ds(slots, slots), :]),
                (w_residual_far.at[pl.ds(0, w_residual_ref.shape[0])], w_residual_ref),
            )
        )
    ]
    for copy in copies:
        copy.start()
    for copy in copies[:5]:
        copy.wait()
    pre_ref[...] = matmul(edge_ref[...], w_edge_ref[...])
    grown = w_grow_ref.shape[0]
    for first in range(0, w_bilinear_ref.shape[1], 2 * narrow):
        pair = [
            w_bilinear_ref[:, at : at + narrow].astype(f32).T for at in (first, first + narrow)
        ]
        if first < grown:
            w_grow_ref[first : first + 2 * narrow, :] = jnp.concatenate(pair, axis=0).astype(bf16)
        else:
            w_mix_ref[:, first - grown : first - grown + 2 * narrow] = jnp.concatenate(
                pair, axis=1
            ).astype(bf16)
    hot = lax.broadcasted_iota(jnp.int32, source_hot_ref.shape[::-1], 0) == source_ref[...]
    source_hot_ref[...] = hot.astype(f32).T.astype(bf16)
    hot = lax.broadcasted_iota(jnp.int32, (atoms, target_ref.shape[1]), 0) == target_ref[...]
    atom_rows_ref[atoms:, :] = hot.astype(f32).astype(bf16)
    for copy in copies[5:]:
        copy.wait()


def main_kernel(
    recv_ref,
    edge_ref,
    pre_ref,
    source_hot_ref,
    w_mix_ref,
    w_grow_ref,
    w_source_ref,
    w_narrow_ref,
    index_ref,
    w_residual_ref,
    atom_rows_ref,
    w_last_far,
    w_atom_far,
    edge_out_ref,
    atom_out_ref,
    w_last_ref,
    w_atom_ref,
    sems,
):
    copies = [
        pltpu.make_async_copy(w_last_far.at[w_residual_ref.shape[0]], w_last_ref, sems.at[0]),
        pltpu.make_async_copy(w_atom_far, w_atom_ref, sems.at[1]),
    ]
    for copy in copies:
        copy.start()
    bf16, f32 = jnp.bfloat16, jnp.float32
    peers = recv_ref.shape[0]
    slot_rows = index_ref.shape[0] // 2
    pieces = slot_rows // peers
    width = pieces * LANES
    edge_count = edge_ref.shape[0]
    proj_width = w_mix_ref.shape[0]
    atom_count = atom_out_ref.shape[0]
    grown = w_grow_ref.shape[0] // proj_width
    basis_rows = w_mix_ref.shape[1] // proj_width + grown
    index_row = basis_rows * pieces
    atom_row = index_row + 2 * pieces
    halves = atom_out_ref.shape[1] // LANES
    cap_a = (recv_ref.shape[1] - atom_row) // halves

    arrived = jnp.concatenate(
        [
            jnp.concatenate(
                [
                    recv_ref[s, atom_row + h * cap_a : atom_row + (h + 1) * cap_a, :]
                    for s in range(peers)
                ],
                axis=0,
            )
            for h in range(halves)
        ],
        axis=1,
    )
    src_rows = matmul(source_hot_ref[...], arrived).astype(bf16)
    edge = edge_ref[...]
    activated = silu(pre_ref[...] + matmul(src_rows, w_source_ref[...])).astype(bf16)
    projected = silu(
        lax.dot_general(
            w_narrow_ref[:proj_width, :], activated, (((1,), (1,)), ((), ())), preferred_element_type=f32
        )
    ).astype(bf16)
    w_mix = w_mix_ref[...]
    table = jnp.concatenate(
        [projected, matmul(w_grow_ref[...], projected).astype(bf16)], axis=0
    )

    edge_iota = lax.broadcasted_iota(jnp.int32, (edge_count, LANES), 0).astype(f32).astype(bf16)
    packed = 16
    upper = lax.broadcasted_iota(jnp.int32, (2 * pieces, LANES), 0) < pieces
    one, zero = jnp.ones((), bf16), jnp.zeros((), bf16)

    def one_hot(rows):
        parts = []
        for piece in range(pieces):
            spread = jnp.broadcast_to(rows[piece : piece + 1, :], (packed, LANES)).astype(bf16)
            spread = jnp.concatenate([spread] * (edge_count // packed), axis=0)
            parts.append(jnp.where(spread == edge_iota, one, zero))
        return jnp.concatenate(parts, axis=1)

    middle = ((edge.astype(f32) + activated.astype(f32)) * inv_root).astype(bf16)
    inner, stage = None, 0

    def basis_of(t):
        return jnp.concatenate(
            [
                recv_ref[t, piece * basis_rows : (piece + 1) * basis_rows, :]
                for piece in range(pieces)
            ],
            axis=1,
        )

    def choose(t):
        slots = recv_ref[t, index_row:atom_row, :].astype(f32).astype(jnp.int32) + width // 2
        lane, row = slots % LANES, slots // LANES
        found = jnp.zeros(slots.shape, jnp.int32)
        for r in range(pieces):
            here = t * pieces + r
            places = jnp.where(
                upper,
                jnp.broadcast_to(index_ref[here : here + 1, :], slots.shape),
                jnp.broadcast_to(
                    index_ref[slot_rows + here : slot_rows + here + 1, :], slots.shape
                ),
            )
            got = jnp.take_along_axis(places, lane, axis=1, mode="promise_in_bounds")
            found = jnp.where(row == r, got, found)
        found = found.astype(f32)
        rows = matmul(table, one_hot(found[:pieces]))
        near = None
        coeffs = basis_of(t)
        for k in range(grown):
            term = rows[(k + 1) * proj_width : (k + 2) * proj_width, :] * coeffs[
                k : k + 1, :
            ].astype(f32)
            near = term if near is None else near + term
        return rows[:proj_width].astype(bf16), one_hot(found[pieces:]), near

    def mix(t, rows, near):
        coeffs = basis_of(t)
        terms = jnp.concatenate(
            [rows * coeffs[k : k + 1, :] for k in range(grown, basis_rows)], axis=0
        )
        return (matmul(w_mix, terms) + near).astype(bf16)

    def spread(mixed, targets):
        return lax.dot_general(
            targets, mixed, (((1,), (1,)), ((), ())), preferred_element_type=f32
        )

    total = jnp.zeros((edge_count, proj_width), f32)
    chosen, mixes = {}, {}
    for step in range(peers + 2):
        if step < peers:
            chosen[step] = choose(step)
        if 0 <= step - 1 < peers:
            mixes[step - 1] = mix(step - 1, chosen[step - 1][0], chosen[step - 1][2])
        if 0 <= step - 2 < peers:
            total = total + spread(mixes.pop(step - 2), chosen.pop(step - 2)[1])
        if step < peers and (step + 1) * w_residual_ref.shape[0] // peers > stage:
            fresh = silu(matmul(middle if stage % 2 == 0 else inner, w_residual_ref[stage]))
            if stage % 2 == 0:
                inner = fresh.astype(bf16)
            else:
                middle = ((middle.astype(f32) + fresh) * inv_root).astype(bf16)
            stage += 1
    for copy in copies:
        copy.wait()
    chain = (middle.astype(f32) + silu(matmul(inner, w_last_ref[...]))) * inv_root
    update = silu(matmul(total.astype(bf16), w_narrow_ref[proj_width:, :]))
    edge_out = (chain + update).astype(bf16)
    edge_out_ref[...] = edge_out
    contrib = matmul(edge_out, w_atom_ref[...]).astype(bf16)
    atom_sum = matmul(atom_rows_ref[atom_count:, :], contrib)
    atom_out_ref[...] = (
        atom_rows_ref[:atom_count, :].astype(f32) + silu(0.25 * atom_sum)
    ).astype(bf16)


def local_blocks(
    peers,
    edge_state,
    atom_state,
    atom_sends,
    edge_source,
    edge_target,
    send_edges,
    triplet_in,
    triplet_out,
    triplet_valid,
    triplet_basis,
    return_edges,
    w_edge,
    w_source,
    w_down,
    w_bilinear,
    w_up,
    w_residual,
    w_atom,
):
    bf16 = jnp.bfloat16
    pieces = WIN // LANES
    rows = triplet_basis.shape[0] * pieces + 2 * pieces
    rows += atom_sends.shape[0] // peers * (atom_state.shape[1] // LANES)
    by_lanes = lambda array: array.reshape(-1, LANES)
    packed = pl.pallas_call(
        pack_kernel,
        out_shape=jax.ShapeDtypeStruct((peers, rows, LANES), bf16),
        name="pack",
    )(
        triplet_basis,
        by_lanes(triplet_valid),
        by_lanes(triplet_in),
        by_lanes(triplet_out),
        atom_state,
        atom_sends[None, :],
    )
    received = lax.all_to_all(packed, "graph", split_axis=0, concat_axis=0, tiled=True)
    like = lambda array: jax.ShapeDtypeStruct(array.shape, array.dtype)
    stay = lambda arrays: [pltpu.with_memory_space_constraint(one, pltpu.HBM) for one in arrays]
    near, far = pl.BlockSpec(memory_space=pltpu.VMEM), pl.BlockSpec(memory_space=pltpu.HBM)
    source, w_down_t = edge_source[None, :], w_down.T
    target, send_edges, return_edges = (
        edge_target[None, :],
        by_lanes(send_edges),
        by_lanes(return_edges),
    )
    edges, atoms = edge_state.shape[0], atom_state.shape[0]
    narrow = w_up.shape[0]
    grown = GROWN * narrow
    early = pl.pallas_call(
        ahead_kernel,
        in_specs=[far] * 12,
        out_specs=[near] * 10,
        out_shape=(
            like(edge_state),
            jax.ShapeDtypeStruct((edges, w_edge.shape[1]), jnp.float32),
            jax.ShapeDtypeStruct((edges, atom_sends.shape[0]), bf16),
            jax.ShapeDtypeStruct((narrow, w_bilinear.shape[1] - grown), bf16),
            jax.ShapeDtypeStruct((grown, narrow), bf16),
            like(w_source),
            jax.ShapeDtypeStruct((2 * w_up.shape[0], w_up.shape[1]), bf16),
            jax.ShapeDtypeStruct((2 * send_edges.shape[0], LANES), jnp.int32),
            jax.ShapeDtypeStruct((w_residual.shape[0] - 1,) + w_residual.shape[1:], bf16),
            jax.ShapeDtypeStruct((2 * atoms, atom_state.shape[1]), bf16),
        ),
        scratch_shapes=[
            pltpu.VMEM(array.shape, array.dtype) for array in (w_edge, source, w_bilinear, target)
        ]
        + [pltpu.SemaphoreType.DMA((12,))],
        compiler_params=pltpu.CompilerParams(vmem_limit_bytes=8 * 1024 * 1024),
        name="ahead",
    )(
        *stay(
            (
                edge_state,
                w_edge,
                source,
                w_bilinear,
                target,
                atom_state,
                w_source,
                w_down_t,
                send_edges,
                return_edges,
                w_up,
                w_residual,
            )
        )
    )
    return pl.pallas_call(
        main_kernel,
        in_specs=[near] * 11 + [far] * 2,
        out_shape=(like(edge_state), like(atom_state)),
        scratch_shapes=[
            pltpu.VMEM(w_residual.shape[1:], bf16),
            pltpu.VMEM(w_atom.shape, bf16),
            pltpu.SemaphoreType.DMA((2,)),
        ],
        compiler_params=pltpu.CompilerParams(vmem_limit_bytes=32 * 1024 * 1024),
        name="block",
    )(received, *early, *stay((w_residual, w_atom)))


def bilinear_terms(inputs_x, coeffs, keeps, w_bilinear):
    expanded = matmul(inputs_x, w_bilinear)
    expanded = expanded.reshape(inputs_x.shape[0], coeffs.shape[0], -1)
    mixed = jnp.einsum("tkd,kt->td", expanded, coeffs.astype(jnp.float32))
    return mixed * keeps.astype(jnp.float32)[:, None]


def tile_sums(slot_rows, local_in, local_out, keeps, coeffs, w_bilinear):
    trip_count = slot_rows.shape[0]
    block_size = WIN
    block_count = trip_count // block_size
    basis_rows = coeffs.shape[0]
    block_iota = jnp.arange(block_size, dtype=jnp.int32)

    def one_block(operands):
        rows_blk, in_blk, out_blk, keep_blk, coef_blk = operands
        in_hot = ((in_blk % block_size)[:, None] == block_iota[None, :]).astype(jnp.bfloat16)
        inputs_x = matmul(in_hot, rows_blk).astype(jnp.bfloat16)
        mixed = bilinear_terms(inputs_x, coef_blk, keep_blk, w_bilinear)
        out_hot = (block_iota[:, None] == (out_blk % block_size)[None, :]).astype(jnp.float32)
        return jnp.dot(
            out_hot, mixed, precision=lax.Precision.HIGHEST, preferred_element_type=jnp.float32
        )

    shaped_coeffs = jnp.transpose(coeffs.reshape(basis_rows, block_count, block_size), (1, 0, 2))
    summed = lax.map(
        one_block,
        (
            slot_rows.reshape(block_count, block_size, -1),
            local_in.reshape(block_count, block_size),
            local_out.reshape(block_count, block_size),
            keeps.reshape(block_count, block_size),
            shaped_coeffs,
        ),
    )
    return summed.reshape(trip_count, -1).astype(jnp.bfloat16)


def on_tiles(
    edge_state,
    atom_state,
    atom_sends,
    edge_source,
    edge_target,
    send_edges,
    triplet_in,
    triplet_out,
    triplet_valid,
    triplet_basis,
    return_edges,
    w_edge,
    w_source,
    w_down,
    w_bilinear,
    w_up,
    w_residual,
    w_atom,
):
    edge_count = edge_state.shape[0]
    atom_count = atom_state.shape[0]
    arrived_atoms = lax.all_to_all(
        pick_rows(atom_sends, atom_state), "graph", split_axis=0, concat_axis=0, tiled=True
    )
    src_rows = pick_rows(edge_source, arrived_atoms)
    pre_act = matmul(edge_state, w_edge) + matmul(src_rows, w_source)
    activated = jax.nn.silu(pre_act).astype(jnp.bfloat16)
    projected = jax.nn.silu(matmul(activated, w_down)).astype(jnp.bfloat16)
    slot_rows = lax.all_to_all(
        pick_rows(send_edges, projected), "graph", split_axis=0, concat_axis=0, tiled=True
    )
    slot_sums = tile_sums(
        slot_rows, triplet_in, triplet_out, triplet_valid, triplet_basis, w_bilinear
    )
    returned = lax.all_to_all(slot_sums, "graph", split_axis=0, concat_axis=0, tiled=True)
    back_hot = (jnp.arange(edge_count, dtype=jnp.int32)[:, None] == return_edges[None, :]).astype(
        jnp.bfloat16
    )
    aggregate = matmul(back_hot, returned)
    update = jax.nn.silu(matmul(aggregate.astype(jnp.bfloat16), w_up))
    base = ((edge_state.astype(jnp.float32) + activated.astype(jnp.float32)) * inv_root).astype(
        jnp.bfloat16
    )
    inner_one = jax.nn.silu(matmul(base, w_residual[0])).astype(jnp.bfloat16)
    middle = (
        (base.astype(jnp.float32) + jax.nn.silu(matmul(inner_one, w_residual[1]))) * inv_root
    ).astype(jnp.bfloat16)
    inner_two = jax.nn.silu(matmul(middle, w_residual[2])).astype(jnp.bfloat16)
    chain = (middle.astype(jnp.float32) + jax.nn.silu(matmul(inner_two, w_residual[3]))) * inv_root
    edge_out = (chain + update).astype(jnp.bfloat16)
    contrib = matmul(edge_out, w_atom).astype(jnp.bfloat16)
    one_hot = (edge_target[None, :] == jnp.arange(atom_count, dtype=jnp.int32)[:, None]).astype(
        jnp.bfloat16
    )
    atom_sum = matmul(one_hot, contrib)
    atom_out = (atom_state.astype(jnp.float32) + jax.nn.silu(0.25 * atom_sum)).astype(jnp.bfloat16)
    return (edge_out, atom_out)


def on_device(*arguments):
    peers = lax.axis_size("graph")
    if arguments[5].shape[0] == peers * WIN:
        return local_blocks(peers, *arguments)
    return on_tiles(*arguments)


def solution(mesh):
    placed = (
        P(("groups", "graph"), None),
        P(("groups", "graph"), None),
        P(("groups", "graph")),
        P(("groups", "graph")),
        P(("groups", "graph")),
        P(("groups", "graph")),
        P(("groups", "graph")),
        P(("groups", "graph")),
        P(("groups", "graph")),
        P(None, ("groups", "graph")),
        P(("groups", "graph")),
        P(),
        P(),
        P(),
        P(),
        P(),
        P(),
        P(),
    )
    return jax.shard_map(
        on_device,
        mesh=mesh,
        in_specs=placed,
        out_specs=(P(("groups", "graph"), None), P(("groups", "graph"), None)),
        check_vma=False,
    )
```

```python
import jax
import jax.numpy as jnp
from jax import lax
from jax.experimental import pallas as pl
from jax.experimental.pallas import tpu as pltpu
from jax.sharding import PartitionSpec as P

WIN = 512
LANES = 128
GROWN = 6


inv_root = 0.7071067811865476


def matmul(left, right):
    return jnp.dot(left, right, preferred_element_type=jnp.float32)


def pick_rows(indices, table):
    chooser = (indices[:, None] == jnp.arange(table.shape[0], dtype=jnp.int32)[None, :]).astype(
        table.dtype
    )
    return matmul(chooser, table).astype(table.dtype)


def silu(v):
    return (0.5 * v) * (1.0 + jnp.tanh(0.5 * v))


def pack_kernel(basis_ref, valid_ref, in_ref, out_ref, atom_ref, sends_ref, send_ref):
    basis_rows = basis_ref.shape[0]
    peers = send_ref.shape[0]
    pieces = valid_ref.shape[0] // peers
    width = pieces * LANES
    atom_slots = sends_ref.shape[1]
    cap_a = atom_slots // peers
    chooser = (
        lax.broadcasted_iota(jnp.int32, (atom_ref.shape[0], atom_slots), 0) == sends_ref[...]
    ).astype(jnp.float32).astype(jnp.bfloat16)
    rows = lax.dot_general(
        chooser, atom_ref[...], (((0,), (0,)), ((), ())), preferred_element_type=jnp.float32
    ).astype(jnp.bfloat16)
    keeps = valid_ref[...].astype(jnp.float32)
    half = width // 2
    local_in = ((in_ref[...] % width) - half).astype(jnp.float32).astype(jnp.bfloat16)
    local_out = ((out_ref[...] % width) - half).astype(jnp.float32).astype(jnp.bfloat16)
    for peer in range(peers):
        parts = []
        for piece in range(pieces):
            row = peer * pieces + piece
            tile = basis_ref[:, row * LANES : (row + 1) * LANES].astype(jnp.float32)
            parts.append((tile * keeps[row : row + 1, :]).astype(jnp.bfloat16))
        parts.append(local_in[peer * pieces : (peer + 1) * pieces, :])
        parts.append(local_out[peer * pieces : (peer + 1) * pieces, :])
        for first in range(0, atom_ref.shape[1], LANES):
            parts.append(rows[peer * cap_a : (peer + 1) * cap_a, first : first + LANES])
        send_ref[peer] = jnp.concatenate(parts, axis=0)


def ahead_kernel(
    edge_far,
    w_edge_far,
    source_far,
    w_bilinear_far,
    target_far,
    atom_far,
    w_source_far,
    w_down_t_far,
    send_far,
    return_far,
    w_up_far,
    w_residual_far,
    edge_ref,
    pre_ref,
    source_hot_ref,
    w_mix_ref,
    w_grow_ref,
    w_source_ref,
    w_narrow_ref,
    index_ref,
    w_residual_ref,
    atom_rows_ref,
    w_edge_ref,
    source_ref,
    w_bilinear_ref,
    target_ref,
    sems,
):
    f32, bf16 = jnp.float32, jnp.bfloat16
    slots, narrow, atoms = send_far.shape[0], w_down_t_far.shape[0], atom_far.shape[0]
    copies = [
        pltpu.make_async_copy(here, there, sems.at[at])
        for at, (here, there) in enumerate(
            (
                (edge_far, edge_ref),
                (w_edge_far, w_edge_ref),
                (source_far, source_ref),
                (w_bilinear_far, w_bilinear_ref),
                (target_far, target_ref),
                (atom_far, atom_rows_ref.at[pl.ds(0, atoms), :]),
                (w_source_far, w_source_ref),
                (w_down_t_far, w_narrow_ref.at[pl.ds(0, narrow), :]),
                (w_up_far, w_narrow_ref.at[pl.ds(narrow, narrow), :]),
                (send_far, index_ref.at[pl.ds(0, slots), :]),
                (return_far, index_ref.at[pl.ds(slots, slots), :]),
                (w_residual_far.at[pl.ds(0, w_residual_ref.shape[0])], w_residual_ref),
            )
        )
    ]
    for copy in copies:
        copy.start()
    for copy in copies[:5]:
        copy.wait()
    pre_ref[...] = matmul(edge_ref[...], w_edge_ref[...])
    grown = w_grow_ref.shape[0]
    for first in range(0, w_bilinear_ref.shape[1], 2 * narrow):
        pair = [
            w_bilinear_ref[:, at : at + narrow].astype(f32).T for at in (first, first + narrow)
        ]
        if first < grown:
            w_grow_ref[first : first + 2 * narrow, :] = jnp.concatenate(pair, axis=0).astype(bf16)
        else:
            w_mix_ref[:, first - grown : first - grown + 2 * narrow] = jnp.concatenate(
                pair, axis=1
            ).astype(bf16)
    hot = lax.broadcasted_iota(jnp.int32, source_hot_ref.shape[::-1], 0) == source_ref[...]
    source_hot_ref[...] = hot.astype(f32).T.astype(bf16)
    hot = lax.broadcasted_iota(jnp.int32, (atoms, target_ref.shape[1]), 0) == target_ref[...]
    atom_rows_ref[atoms:, :] = hot.astype(f32).astype(bf16)
    for copy in copies[5:]:
        copy.wait()


def main_kernel(
    recv_ref,
    edge_ref,
    pre_ref,
    source_hot_ref,
    w_mix_ref,
    w_grow_ref,
    w_source_ref,
    w_narrow_ref,
    index_ref,
    w_residual_ref,
    atom_rows_ref,
    w_last_far,
    w_atom_far,
    edge_out_ref,
    atom_out_ref,
    w_last_ref,
    w_atom_ref,
    sems,
):
    copies = [
        pltpu.make_async_copy(w_last_far.at[w_residual_ref.shape[0]], w_last_ref, sems.at[0]),
        pltpu.make_async_copy(w_atom_far, w_atom_ref, sems.at[1]),
    ]
    for copy in copies:
        copy.start()
    bf16, f32 = jnp.bfloat16, jnp.float32
    peers = recv_ref.shape[0]
    slot_rows = index_ref.shape[0] // 2
    pieces = slot_rows // peers
    width = pieces * LANES
    edge_count = edge_ref.shape[0]
    proj_width = w_mix_ref.shape[0]
    atom_count = atom_out_ref.shape[0]
    grown = w_grow_ref.shape[0] // proj_width
    basis_rows = w_mix_ref.shape[1] // proj_width + grown
    index_row = basis_rows * pieces
    atom_row = index_row + 2 * pieces
    halves = atom_out_ref.shape[1] // LANES
    cap_a = (recv_ref.shape[1] - atom_row) // halves

    arrived = jnp.concatenate(
        [
            jnp.concatenate(
                [
                    recv_ref[s, atom_row + h * cap_a : atom_row + (h + 1) * cap_a, :]
                    for s in range(peers)
                ],
                axis=0,
            )
            for h in range(halves)
        ],
        axis=1,
    )
    src_rows = matmul(source_hot_ref[...], arrived).astype(bf16)
    edge = edge_ref[...]
    activated = silu(pre_ref[...] + matmul(src_rows, w_source_ref[...])).astype(bf16)
    projected = silu(
        lax.dot_general(
            w_narrow_ref[:proj_width, :], activated, (((1,), (1,)), ((), ())), preferred_element_type=f32
        )
    ).astype(bf16)
    w_mix = w_mix_ref[...]
    table = jnp.concatenate(
        [projected, matmul(w_grow_ref[...], projected).astype(bf16)], axis=0
    )

    edge_iota = lax.broadcasted_iota(jnp.int32, (edge_count, LANES), 0).astype(f32).astype(bf16)
    packed = 16
    upper = lax.broadcasted_iota(jnp.int32, (2 * pieces, LANES), 0) < pieces
    one, zero = jnp.ones((), bf16), jnp.zeros((), bf16)

    def one_hot(rows):
        parts = []
        for piece in range(pieces):
            spread = jnp.broadcast_to(rows[piece : piece + 1, :], (packed, LANES)).astype(bf16)
            spread = jnp.concatenate([spread] * (edge_count // packed), axis=0)
            parts.append(jnp.where(spread == edge_iota, one, zero))
        return jnp.concatenate(parts, axis=1)

    middle = ((edge.astype(f32) + activated.astype(f32)) * inv_root).astype(bf16)
    inner, stage = None, 0

    def basis_of(t):
        return jnp.concatenate(
            [
                recv_ref[t, piece * basis_rows : (piece + 1) * basis_rows, :]
                for piece in range(pieces)
            ],
            axis=1,
        )

    def choose(t):
        slots = recv_ref[t, index_row:atom_row, :].astype(f32).astype(jnp.int32) + width // 2
        lane, row = slots % LANES, slots // LANES
        found = jnp.zeros(slots.shape, jnp.int32)
        for r in range(pieces):
            here = t * pieces + r
            places = jnp.where(
                upper,
                jnp.broadcast_to(index_ref[here : here + 1, :], slots.shape),
                jnp.broadcast_to(
                    index_ref[slot_rows + here : slot_rows + here + 1, :], slots.shape
                ),
            )
            got = jnp.take_along_axis(places, lane, axis=1, mode="promise_in_bounds")
            found = jnp.where(row == r, got, found)
        found = found.astype(f32)
        return one_hot(found[:pieces]), one_hot(found[pieces:])

    def gather(t, hot, targets):
        rows = matmul(table, hot)
        near = None
        coeffs = basis_of(t)
        for k in range(grown):
            term = rows[(k + 1) * proj_width : (k + 2) * proj_width, :] * coeffs[
                k : k + 1, :
            ].astype(f32)
            near = term if near is None else near + term
        return rows[:proj_width].astype(bf16), targets, near

    def mix(t, rows, near):
        coeffs = basis_of(t)
        terms = jnp.concatenate(
            [rows * coeffs[k : k + 1, :] for k in range(grown, basis_rows)], axis=0
        )
        return (matmul(w_mix, terms) + near).astype(bf16)

    def spread(mixed, targets):
        return lax.dot_general(
            targets, mixed, (((1,), (1,)), ((), ())), preferred_element_type=f32
        )

    total = jnp.zeros((edge_count, proj_width), f32)
    chosen, mixes, hots = {}, {}, {}
    for step in range(peers + 2):
        if step == 0:
            hots[0] = choose(0)
        if step + 1 < peers:
            hots[step + 1] = choose(step + 1)
        if step < peers:
            chosen[step] = gather(step, *hots.pop(step))
        if 0 <= step - 1 < peers:
            mixes[step - 1] = mix(step - 1, chosen[step - 1][0], chosen[step - 1][2])
        if 0 <= step - 2 < peers:
            total = total + spread(mixes.pop(step - 2), chosen.pop(step - 2)[1])
        if step < peers and (step + 1) * w_residual_ref.shape[0] // peers > stage:
            fresh = silu(matmul(middle if stage % 2 == 0 else inner, w_residual_ref[stage]))
            if stage % 2 == 0:
                inner = fresh.astype(bf16)
            else:
                middle = ((middle.astype(f32) + fresh) * inv_root).astype(bf16)
            stage += 1
    for copy in copies:
        copy.wait()
    chain = (middle.astype(f32) + silu(matmul(inner, w_last_ref[...]))) * inv_root
    update = silu(matmul(total.astype(bf16), w_narrow_ref[proj_width:, :]))
    edge_out = (chain + update).astype(bf16)
    edge_out_ref[...] = edge_out
    contrib = matmul(edge_out, w_atom_ref[...]).astype(bf16)
    atom_sum = matmul(atom_rows_ref[atom_count:, :], contrib)
    atom_out_ref[...] = (
        atom_rows_ref[:atom_count, :].astype(f32) + silu(0.25 * atom_sum)
    ).astype(bf16)


def local_blocks(
    peers,
    edge_state,
    atom_state,
    atom_sends,
    edge_source,
    edge_target,
    send_edges,
    triplet_in,
    triplet_out,
    triplet_valid,
    triplet_basis,
    return_edges,
    w_edge,
    w_source,
    w_down,
    w_bilinear,
    w_up,
    w_residual,
    w_atom,
):
    bf16 = jnp.bfloat16
    pieces = WIN // LANES
    rows = triplet_basis.shape[0] * pieces + 2 * pieces
    rows += atom_sends.shape[0] // peers * (atom_state.shape[1] // LANES)
    by_lanes = lambda array: array.reshape(-1, LANES)
    packed = pl.pallas_call(
        pack_kernel,
        out_shape=jax.ShapeDtypeStruct((peers, rows, LANES), bf16),
        name="pack",
    )(
        triplet_basis,
        by_lanes(triplet_valid),
        by_lanes(triplet_in),
        by_lanes(triplet_out),
        atom_state,
        atom_sends[None, :],
    )
    received = lax.all_to_all(packed, "graph", split_axis=0, concat_axis=0, tiled=True)
    like = lambda array: jax.ShapeDtypeStruct(array.shape, array.dtype)
    stay = lambda arrays: [pltpu.with_memory_space_constraint(one, pltpu.HBM) for one in arrays]
    near, far = pl.BlockSpec(memory_space=pltpu.VMEM), pl.BlockSpec(memory_space=pltpu.HBM)
    source, w_down_t = edge_source[None, :], w_down.T
    target, send_edges, return_edges = (
        edge_target[None, :],
        by_lanes(send_edges),
        by_lanes(return_edges),
    )
    edges, atoms = edge_state.shape[0], atom_state.shape[0]
    narrow = w_up.shape[0]
    grown = GROWN * narrow
    early = pl.pallas_call(
        ahead_kernel,
        in_specs=[far] * 12,
        out_specs=[near] * 10,
        out_shape=(
            like(edge_state),
            jax.ShapeDtypeStruct((edges, w_edge.shape[1]), jnp.float32),
            jax.ShapeDtypeStruct((edges, atom_sends.shape[0]), bf16),
            jax.ShapeDtypeStruct((narrow, w_bilinear.shape[1] - grown), bf16),
            jax.ShapeDtypeStruct((grown, narrow), bf16),
            like(w_source),
            jax.ShapeDtypeStruct((2 * w_up.shape[0], w_up.shape[1]), bf16),
            jax.ShapeDtypeStruct((2 * send_edges.shape[0], LANES), jnp.int32),
            jax.ShapeDtypeStruct((w_residual.shape[0] - 1,) + w_residual.shape[1:], bf16),
            jax.ShapeDtypeStruct((2 * atoms, atom_state.shape[1]), bf16),
        ),
        scratch_shapes=[
            pltpu.VMEM(array.shape, array.dtype) for array in (w_edge, source, w_bilinear, target)
        ]
        + [pltpu.SemaphoreType.DMA((12,))],
        compiler_params=pltpu.CompilerParams(vmem_limit_bytes=8 * 1024 * 1024),
        name="ahead",
    )(
        *stay(
            (
                edge_state,
                w_edge,
                source,
                w_bilinear,
                target,
                atom_state,
                w_source,
                w_down_t,
                send_edges,
                return_edges,
                w_up,
                w_residual,
            )
        )
    )
    return pl.pallas_call(
        main_kernel,
        in_specs=[near] * 11 + [far] * 2,
        out_shape=(like(edge_state), like(atom_state)),
        scratch_shapes=[
            pltpu.VMEM(w_residual.shape[1:], bf16),
            pltpu.VMEM(w_atom.shape, bf16),
            pltpu.SemaphoreType.DMA((2,)),
        ],
        compiler_params=pltpu.CompilerParams(vmem_limit_bytes=32 * 1024 * 1024),
        name="block",
    )(received, *early, *stay((w_residual, w_atom)))


def bilinear_terms(inputs_x, coeffs, keeps, w_bilinear):
    expanded = matmul(inputs_x, w_bilinear)
    expanded = expanded.reshape(inputs_x.shape[0], coeffs.shape[0], -1)
    mixed = jnp.einsum("tkd,kt->td", expanded, coeffs.astype(jnp.float32))
    return mixed * keeps.astype(jnp.float32)[:, None]


def tile_sums(slot_rows, local_in, local_out, keeps, coeffs, w_bilinear):
    trip_count = slot_rows.shape[0]
    block_size = WIN
    block_count = trip_count // block_size
    basis_rows = coeffs.shape[0]
    block_iota = jnp.arange(block_size, dtype=jnp.int32)

    def one_block(operands):
        rows_blk, in_blk, out_blk, keep_blk, coef_blk = operands
        in_hot = ((in_blk % block_size)[:, None] == block_iota[None, :]).astype(jnp.bfloat16)
        inputs_x = matmul(in_hot, rows_blk).astype(jnp.bfloat16)
        mixed = bilinear_terms(inputs_x, coef_blk, keep_blk, w_bilinear)
        out_hot = (block_iota[:, None] == (out_blk % block_size)[None, :]).astype(jnp.float32)
        return jnp.dot(
            out_hot, mixed, precision=lax.Precision.HIGHEST, preferred_element_type=jnp.float32
        )

    shaped_coeffs = jnp.transpose(coeffs.reshape(basis_rows, block_count, block_size), (1, 0, 2))
    summed = lax.map(
        one_block,
        (
            slot_rows.reshape(block_count, block_size, -1),
            local_in.reshape(block_count, block_size),
            local_out.reshape(block_count, block_size),
            keeps.reshape(block_count, block_size),
            shaped_coeffs,
        ),
    )
    return summed.reshape(trip_count, -1).astype(jnp.bfloat16)


def on_tiles(
    edge_state,
    atom_state,
    atom_sends,
    edge_source,
    edge_target,
    send_edges,
    triplet_in,
    triplet_out,
    triplet_valid,
    triplet_basis,
    return_edges,
    w_edge,
    w_source,
    w_down,
    w_bilinear,
    w_up,
    w_residual,
    w_atom,
):
    edge_count = edge_state.shape[0]
    atom_count = atom_state.shape[0]
    arrived_atoms = lax.all_to_all(
        pick_rows(atom_sends, atom_state), "graph", split_axis=0, concat_axis=0, tiled=True
    )
    src_rows = pick_rows(edge_source, arrived_atoms)
    pre_act = matmul(edge_state, w_edge) + matmul(src_rows, w_source)
    activated = jax.nn.silu(pre_act).astype(jnp.bfloat16)
    projected = jax.nn.silu(matmul(activated, w_down)).astype(jnp.bfloat16)
    slot_rows = lax.all_to_all(
        pick_rows(send_edges, projected), "graph", split_axis=0, concat_axis=0, tiled=True
    )
    slot_sums = tile_sums(
        slot_rows, triplet_in, triplet_out, triplet_valid, triplet_basis, w_bilinear
    )
    returned = lax.all_to_all(slot_sums, "graph", split_axis=0, concat_axis=0, tiled=True)
    back_hot = (jnp.arange(edge_count, dtype=jnp.int32)[:, None] == return_edges[None, :]).astype(
        jnp.bfloat16
    )
    aggregate = matmul(back_hot, returned)
    update = jax.nn.silu(matmul(aggregate.astype(jnp.bfloat16), w_up))
    base = ((edge_state.astype(jnp.float32) + activated.astype(jnp.float32)) * inv_root).astype(
        jnp.bfloat16
    )
    inner_one = jax.nn.silu(matmul(base, w_residual[0])).astype(jnp.bfloat16)
    middle = (
        (base.astype(jnp.float32) + jax.nn.silu(matmul(inner_one, w_residual[1]))) * inv_root
    ).astype(jnp.bfloat16)
    inner_two = jax.nn.silu(matmul(middle, w_residual[2])).astype(jnp.bfloat16)
    chain = (middle.astype(jnp.float32) + jax.nn.silu(matmul(inner_two, w_residual[3]))) * inv_root
    edge_out = (chain + update).astype(jnp.bfloat16)
    contrib = matmul(edge_out, w_atom).astype(jnp.bfloat16)
    one_hot = (edge_target[None, :] == jnp.arange(atom_count, dtype=jnp.int32)[:, None]).astype(
        jnp.bfloat16
    )
    atom_sum = matmul(one_hot, contrib)
    atom_out = (atom_state.astype(jnp.float32) + jax.nn.silu(0.25 * atom_sum)).astype(jnp.bfloat16)
    return (edge_out, atom_out)


def on_device(*arguments):
    peers = lax.axis_size("graph")
    if arguments[5].shape[0] == peers * WIN:
        return local_blocks(peers, *arguments)
    return on_tiles(*arguments)


def solution(mesh):
    placed = (
        P(("groups", "graph"), None),
        P(("groups", "graph"), None),
        P(("groups", "graph")),
        P(("groups", "graph")),
        P(("groups", "graph")),
        P(("groups", "graph")),
        P(("groups", "graph")),
        P(("groups", "graph")),
        P(("groups", "graph")),
        P(None, ("groups", "graph")),
        P(("groups", "graph")),
        P(),
        P(),
        P(),
        P(),
        P(),
        P(),
        P(),
    )
    return jax.shard_map(
        on_device,
        mesh=mesh,
        in_specs=placed,
        out_specs=(P(("groups", "graph"), None), P(("groups", "graph"), None)),
        check_vma=False,
    )
```
